256 devices in a mesh: leaf: 16 (over z, core), rep: 16 (over y, x).
Axes of the slice: x: 4, y: 4, z: 8, core: 2. Of those that a mesh axis runs over, the one named last changes fastest.
Arguments:
- curve_coordinates: float32 [2, 131072], P(None, 'leaf'), may hold values from -1.25 to 1.25, as said below
- weighted_density: float32 [131072], P('leaf'), may hold values from 0.02 to 0.2
- random_test_matrix: float32 [128, 131072], P('rep', 'leaf'), may hold values from -6 to 6
- sketch_matrix: float32 [128, 131072], P('rep', 'leaf'), may hold values from -12 to 12
Outputs:
- leaf_basis: float32 [128, 131072], P('rep', 'leaf')
- top_basis: float32 [16, 128, 256], P('leaf', 'rep')
The draws below stay inside these ranges and needn't reach their ends.
Inputs may be any that keep to these rules, and one draw needn't show every extreme that they name: `curve_coordinates`: the points are in order along one closed smooth curve, one point in each of 131072 equal parameter cells.
All inputs are finite; a program needn't handle non-finite values.
Results may differ from the reference program's by a relative error of at most 0.00035.
Values sent between devices are 32-bit elements; how exact they have to be, the bound alone decides.
No kernel may reach another device: no remote copies, remote signals or barrier semaphores. Data moves between devices by JAX's collectives and lax.ppermute only.
A program may use at most 64 MiB of HBM per device.

```python
import math
import jax
import jax.numpy as jnp
from jax import lax

NODES_PER_CELL = 512
S = 128
LEAF_LEVELS = 4
CROSS = 3
CURVE_NODE_NUM = 131072


def draw_curve_coordinates(key, part):
    position = jnp.arange(CURVE_NODE_NUM, dtype=jnp.float32)
    jitter = jax.random.uniform(key, (CURVE_NODE_NUM,), jnp.float32, -0.3, 0.3)
    angle_rad = 2.0 * math.pi * (position + 0.5 + jitter) / CURVE_NODE_NUM
    radius = 1.0 + 0.2 * jnp.cos(5.0 * angle_rad)
    return jnp.stack([radius * jnp.cos(angle_rad), radius * jnp.sin(angle_rad)])


def steps_of(own_key, shape, shards, smallest, top_value):
    loudness = 1.0
    for axis_at, parts in shards:
        steps = jax.random.uniform(jax.random.fold_in(jax.random.fold_in(own_key, 6), axis_at), (parts,), jnp.float32, smallest / len(shards), top_value / len(shards))
        loudness = loudness * jnp.repeat(jnp.exp(steps), shape[axis_at] // parts).reshape((-1,) + (1,) * (len(shape) - 1 - axis_at))
    return loudness


def bell_draw(rng, dims, deviation, reach, split=(), held_as=jnp.bfloat16):
    result = deviation * jax.random.normal(rng, dims, jnp.float32)
    if split:
        result = result * steps_of(rng, dims, split, -0.22, 0.18)
    return jnp.clip(result, -reach, reach).astype(held_as)


def setup_inputs(seed: int = 0) -> dict:
    streams_of = jax.random.split(jax.random.key(seed), 5)
    curve_coordinates = draw_curve_coordinates(jax.random.fold_in(streams_of[4], 71), 0)
    weighted_density = jnp.clip(jnp.exp(math.log(0.2) - 2.3025851 * jax.random.uniform(streams_of[1], (CURVE_NODE_NUM,), jnp.float32) ** steps_of(streams_of[1], (CURVE_NODE_NUM,), ((0, 16),), -0.2, 0.2)), 0.02, 0.2)
    random_test_matrix = bell_draw(streams_of[2], (S, CURVE_NODE_NUM), 1.0, 6.0, ((0, 16), (1, 16)), jnp.float32)
    sketch_matrix = bell_draw(streams_of[3], (S, CURVE_NODE_NUM), 2.0, 12.0, ((0, 16), (1, 16)), jnp.float32)
    return {"curve_coordinates": curve_coordinates, "weighted_density": weighted_density, "random_test_matrix": random_test_matrix, "sketch_matrix": sketch_matrix}


grouping = 4

def distances(targets, sources):
    delta_x = targets[0][:, None] - sources[0][None, :]
    delta_y = targets[1][:, None] - sources[1][None, :]
    return delta_x * delta_x + delta_y * delta_y

def near_field(window, blocks):
    span = window.shape[2]
    height = window.shape[1]
    row_ids = lax.broadcasted_iota(jnp.int32, (span, 3 * span), 0)
    col_ids = lax.broadcasted_iota(jnp.int32, (span, 3 * span), 1)
    same = row_ids + span == col_ids
    results = []
    for offset in range(blocks):
        sources = window[offset:offset + 3].transpose(1, 0, 2).reshape(height, 3 * span)
        targets = window[offset + 1, :2]
        squared = distances(targets, sources[:2])
        guarded = jnp.where(same, 1.0, squared)
        potential = jnp.log(guarded) * (-0.25 / math.pi)
        self_term = (1.0 - jnp.log(0.5 * sources[2])) * (0.5 / math.pi)
        matrix = jnp.where(same, self_term[None, :], potential) * sources[2][None, :]
        results.append(jnp.einsum('cj,ij->ci', sources[3:], matrix, precision=lax.Precision.HIGHEST))
    return jnp.stack(results)

def couple(skel_rows, skel_cols):

    def single(rows, cols):
        return jnp.log(distances(rows[:2], cols[:2])) * (-0.25 / math.pi) * cols[2][None, :]
    return jax.vmap(single)(skel_rows, skel_cols)

def assemble(sample_hat, probe_hat, skeleton):
    upper_y, lower_y = (sample_hat[0::2], sample_hat[1::2])
    upper_w, lower_w = (probe_hat[0::2], probe_hat[1::2])
    upper_s, lower_s = (skeleton[0::2], skeleton[1::2])
    cross_ab = couple(upper_s, lower_s)
    cross_ba = couple(lower_s, upper_s)
    top_rows = upper_y - jnp.einsum('nct,nst->ncs', lower_w, cross_ab, precision=lax.Precision.HIGHEST)
    bottom_rows = lower_y - jnp.einsum('nct,nst->ncs', upper_w, cross_ba, precision=lax.Precision.HIGHEST)
    off_diag = jnp.concatenate([top_rows, bottom_rows], 2)
    joined_y = jnp.concatenate([upper_y, lower_y], 2)
    joined_w = jnp.concatenate([upper_w, lower_w], 2)
    joined_s = jnp.concatenate([upper_s, lower_s], 2)[:, :, ::2]
    parent_s = jnp.concatenate([joined_s[:, :2], 2.0 * joined_s[:, 2:]], 1)
    return (off_diag, joined_y, joined_w, parent_s)

def project(basis_rows, stacked):
    return jnp.einsum('nsm,ncm->ncs', basis_rows, stacked, precision=lax.Precision.HIGHEST)

def orthonormal(off_diag):
    gram = jnp.einsum('nsm,ntm->nst', off_diag, off_diag, precision=lax.Precision.HIGHEST)
    factor = jnp.linalg.cholesky(gram)
    order = gram.shape[1]
    identity = jnp.eye(order, dtype=gram.dtype)
    inverse = jax.vmap(lambda low: jax.scipy.linalg.solve_triangular(low, identity, lower=True))(factor)
    return jnp.einsum('nst,ntm->nsm', inverse, off_diag, precision=lax.Precision.HIGHEST)

def reference(curve_coordinates, weighted_density, random_test_matrix, sketch_matrix):
    total = curve_coordinates.shape[1]
    number_finest_cells = total // NODES_PER_CELL
    step_width = NODES_PER_CELL // S
    finest_cell_coordinates = curve_coordinates.reshape(2, number_finest_cells, NODES_PER_CELL).transpose(1, 0, 2)
    finest_cell_weights = weighted_density.reshape(number_finest_cells, 1, NODES_PER_CELL)
    finest_cell_random_test = random_test_matrix.reshape(S, number_finest_cells, NODES_PER_CELL).transpose(1, 0, 2)
    leaf_y = sketch_matrix.reshape(S, number_finest_cells, NODES_PER_CELL).transpose(1, 0, 2)
    scratch_buffer = jnp.concatenate([finest_cell_coordinates, finest_cell_weights, finest_cell_random_test], 1)
    padded_rows = jnp.concatenate([scratch_buffer[-1:], scratch_buffer, scratch_buffer[:1]], 0)

    def block_near(block_index):
        window = lax.dynamic_slice_in_dim(padded_rows, block_index * grouping, grouping + 2, 0)
        return near_field(window, grouping)
    near = lax.map(block_near, jnp.arange(number_finest_cells // grouping, dtype=jnp.int32))
    near = near.reshape(number_finest_cells, S, NODES_PER_CELL)
    off_diag = leaf_y - near
    basis_rows = orthonormal(off_diag)
    leaf_basis = basis_rows.transpose(1, 0, 2).reshape(S, total) * math.sqrt(NODES_PER_CELL)
    sample_hat = project(basis_rows, leaf_y)
    probe_hat = project(basis_rows, finest_cell_random_test)
    skeleton_unpruned = scratch_buffer[:, :3, ::step_width]
    skeleton = jnp.concatenate([skeleton_unpruned[:, :2], step_width * skeleton_unpruned[:, 2:]], 1)
    for level in range(LEAF_LEVELS + CROSS):
        off_diag, joined_y, joined_w, skeleton = assemble(sample_hat, probe_hat, skeleton)
        basis_rows = orthonormal(off_diag)
        sample_hat = project(basis_rows, joined_y)
        probe_hat = project(basis_rows, joined_w)
    top_basis = jnp.repeat(basis_rows, 2 ** CROSS, axis=0) * math.sqrt(2 * S)
    return (leaf_basis, top_basis)
```

```python
import math

import jax
import jax.numpy as jnp
from jax import lax
from jax.experimental import pallas as pl
from jax.experimental.pallas import tpu as pltpu
from jax.sharding import PartitionSpec as P

LEAF = 512
S = 128
NB = 32
HI = lax.Precision.HIGHEST
LOG_SCALE = -0.25 / math.pi


def dot(a, b, dims):
    return lax.dot_general(
        a, b, (dims, ((), ())), precision=HI, preferred_element_type=jnp.float32
    )


def nn(a, b):
    return dot(a, b, ((1,), (0,)))


def nt(a, b):
    return dot(a, b, ((1,), (1,)))


def tn(a, b):
    return dot(a, b, ((0,), (0,)))


def inverse_factor(block):
    n = block.shape[0]
    rows = lax.broadcasted_iota(jnp.int32, (n, n), 0)
    cols = lax.broadcasted_iota(jnp.int32, (n, n), 1)
    eye = jnp.where(rows == cols, 1.0, 0.0).astype(jnp.float32)
    x = jnp.concatenate([block, eye], 1)
    below = lax.broadcasted_iota(jnp.int32, (n, 1), 0)
    for k in range(n):
        row = x[k : k + 1] * (1.0 / x[k : k + 1, k : k + 1])
        col = jnp.where(below > k, x[:, k : k + 1], 0.0)
        x = x - col * row
    pivots = jnp.sum(jnp.where(rows == cols, x[:, :n], 0.0), 1, keepdims=True)
    return x[:, n:] * lax.rsqrt(pivots)


def eliminate(gram, right):
    n = gram.shape[0]
    whole = jnp.concatenate([gram, right], 1)
    blocks = [whole[i : i + NB] for i in range(0, n, NB)]
    done = []
    for k in range(len(blocks)):
        at = slice(k * NB, (k + 1) * NB)
        upper = nn(inverse_factor(blocks[k][:, at]), blocks[k])
        for j in range(k + 1, len(blocks)):
            blocks[j] = blocks[j] - tn(upper[:, j * NB : (j + 1) * NB], upper)
        done.append(upper[:, n:])
    return jnp.concatenate(done, 0)


def log_distances(cols, rows):
    dx = cols[:, 0:1] - rows[0:1]
    dy = cols[:, 1:2] - rows[1:2]
    return dx * dx + dy * dy


def leaf_kernel(points_ref, data_ref, q_ref, hat_ref):
    points = points_ref[...]
    targets = points[:, LEAF : 2 * LEAF]
    near = jnp.zeros((S, LEAF), jnp.float32)
    for chunk in range(3 * LEAF // S):
        at = slice(chunk * S, (chunk + 1) * S)
        source = points[:, at]
        cols = source.T
        squared = log_distances(cols, targets)
        own = chunk * S - LEAF
        if 0 <= own < LEAF:
            i = lax.broadcasted_iota(jnp.int32, (S, LEAF), 0) + own
            same = i == lax.broadcasted_iota(jnp.int32, (S, LEAF), 1)
            itself = -2.0 * (1.0 - jnp.log(0.5 * cols[:, 2:3]))
            kernel = jnp.where(same, itself, jnp.log(jnp.where(same, 1.0, squared)))
        else:
            kernel = jnp.log(squared)
        tests = data_ref[:, LEAF + chunk * S : LEAF + (chunk + 1) * S]
        near = near + nn(tests * (source[2:3] * LOG_SCALE), kernel)
    samples = data_ref[:, :LEAF]
    z = samples - near
    q = eliminate(nt(z, z), z)
    q_ref[...] = q * math.sqrt(LEAF)
    hat_ref[:S] = nt(q, samples)
    hat_ref[S:] = nt(q, data_ref[:, 2 * LEAF : 3 * LEAF])


def off_diagonal(skel_ref, mine_ref, other_ref):
    mine, other = skel_ref[0], skel_ref[1]
    mine_cols, other_cols = mine.T, other.T
    to_mine = jnp.log(log_distances(mine_cols, other)) * (other[2:3] * LOG_SCALE)
    to_other = jnp.log(log_distances(other_cols, mine)) * (mine[2:3] * LOG_SCALE)
    z_mine = mine_ref[:S] - nn(to_mine, other_ref[S:])
    z_other = other_ref[:S] - nn(to_other, mine_ref[S:])
    return z_mine, z_other


def parent_kernel(skel_ref, mine_ref, other_ref, hat_ref):
    z_mine, z_other = off_diagonal(skel_ref, mine_ref, other_ref)
    gram = tn(z_mine, z_mine) + tn(z_other, z_other)
    right = jnp.concatenate(
        [
            tn(z_mine, mine_ref[:S]) + tn(z_other, other_ref[:S]),
            tn(z_mine, mine_ref[S:]) + tn(z_other, other_ref[S:]),
        ],
        1,
    )
    hat = eliminate(gram, right)
    hat_ref[:S] = hat[:, :S]
    hat_ref[S:] = hat[:, S:]


def top_kernel(second_ref, skel_ref, mine_ref, other_ref, q_ref):
    z_mine, z_other = off_diagonal(skel_ref, mine_ref, other_ref)
    gram = tn(z_mine, z_mine) + tn(z_other, z_other)
    second = second_ref[0] == 1
    first = jnp.where(second, z_other, z_mine)
    last = jnp.where(second, z_mine, z_other)
    q = eliminate(gram, jnp.concatenate([first.T, last.T], 1))
    q_ref[...] = q * math.sqrt(2 * S)


VMEM = pl.BlockSpec(memory_space=pltpu.VMEM)
SMEM = pl.BlockSpec(memory_space=pltpu.SMEM)
PARAMS = pltpu.CompilerParams(vmem_limit_bytes=40 * 1024 * 1024)


def call(kernel, shapes, specs, *operands):
    return pl.pallas_call(
        kernel,
        out_shape=[jax.ShapeDtypeStruct(s, jnp.float32) for s in shapes],
        in_specs=specs,
        out_specs=[VMEM] * len(shapes),
        compiler_params=PARAMS,
    )(*operands)


def swap(block, axis, mask):
    count = lax.axis_size(axis)
    return lax.ppermute(block, axis, [(i, i ^ mask) for i in range(count)])


def with_halo(block, axis, width):
    count = lax.axis_size(axis)
    forward = [(i, (i + 1) % count) for i in range(count)]
    backward = [(i, (i - 1) % count) for i in range(count)]
    low = lax.ppermute(block[:, -width:], axis, forward)
    high = lax.ppermute(block[:, :width], axis, backward)
    return jnp.concatenate([low, block, high], 1)


def node_skeletons(points, level, index, scale):
    nodes = points.shape[1] // (S << level)
    every = points.reshape(3, nodes, S, 1 << level)[..., 0]
    pair = jnp.stack(
        [
            lax.dynamic_index_in_dim(every, index, 1, keepdims=False),
            lax.dynamic_index_in_dim(every, index ^ 1, 1, keepdims=False),
        ]
    )
    pair = jnp.concatenate([pair[:, :2], scale * pair[:, 2:]], 1)
    return jnp.pad(pair, ((0, 0), (0, 5), (0, 0)))


def body(curve_coordinates, weighted_density, random_test_matrix, sketch_matrix):
    columns, width = random_test_matrix.shape
    cells = width // LEAF
    cell_levels = cells.bit_length() - 1
    cross_levels = 3
    rep = lax.axis_index("rep")
    leaf = lax.axis_index("leaf")

    points = jnp.concatenate([curve_coordinates, weighted_density[None]], 0)
    wide = with_halo(jnp.concatenate([points, random_test_matrix], 0), "leaf", LEAF)
    wide_points, wide_tests = wide[:3], wide[3:]
    window = lax.dynamic_slice_in_dim(wide_points, rep * LEAF, 3 * LEAF, 1)
    window = jnp.pad(window, ((0, 5), (0, 0)))
    parcels = jnp.stack(
        [
            jnp.concatenate(
                [
                    sketch_matrix[:, i * LEAF : (i + 1) * LEAF],
                    wide_tests[:, i * LEAF : (i + 3) * LEAF],
                ],
                1,
            )
            for i in range(cells)
        ]
    )
    data = lax.all_to_all(parcels, "rep", 0, 0).reshape(cells * columns, 4 * LEAF)

    skeleton = points[:, :: LEAF // S]
    far = lax.all_gather(skeleton[:, ::cells], "leaf", axis=1, tiled=True)
    step = LEAF // S
    pairs = [
        node_skeletons(skeleton, level, rep >> level, step << level)
        for level in range(cell_levels)
    ]
    pairs += [
        node_skeletons(far, level, leaf >> level, step << (cell_levels + level))
        for level in range(cross_levels)
    ]

    basis, hat = call(
        leaf_kernel, [(S, LEAF), (2 * S, S)], [VMEM, VMEM], window, data
    )
    leaf_basis = lax.all_to_all(basis.reshape(cells, columns, LEAF), "rep", 0, 0)
    leaf_basis = leaf_basis.transpose(1, 0, 2).reshape(columns, width)

    routes = [("rep", 1), ("rep", 3), ("rep", 4), ("rep", 12)]
    routes += [("leaf", 1), ("leaf", 2), ("leaf", 4)]
    for pair, (axis, mask) in zip(pairs[:-1], routes[:-1]):
        other = swap(hat, axis, mask)
        (hat,) = call(parent_kernel, [(2 * S, S)], [VMEM] * 3, pair, hat, other)
    axis, mask = routes[-1]
    other = swap(hat, axis, mask)
    second = (leaf >> (cross_levels - 1) & 1).astype(jnp.int32).reshape(1)
    (top,) = call(
        top_kernel, [(S, 2 * S)], [SMEM] + [VMEM] * 3, second, pairs[-1], hat, other
    )
    mine = lax.dynamic_slice_in_dim(top, rep * columns, columns, 0)
    return (leaf_basis, mine[None])


def solution(mesh):
    return jax.shard_map(
        body,
        mesh=mesh,
        in_specs=(P(None, "leaf"), P("leaf"), P("rep", "leaf"), P("rep", "leaf")),
        out_specs=(P("rep", "leaf"), P("leaf", "rep", None)),
        check_vma=False,
    )
```

```python
import math

import jax
import jax.numpy as jnp
from jax import lax
from jax.experimental import pallas as pl
from jax.experimental.pallas import tpu as pltpu
from jax.sharding import PartitionSpec as P

LEAF = 512
S = 128
NB = 32
SUB = 8
STEP = LEAF // S
F32 = jnp.float32
BF16 = jnp.bfloat16
LOG_SCALE = -0.25 / math.pi


def split3(x):
    high = x.astype(BF16)
    rest = x - high.astype(F32)
    mid = rest.astype(BF16)
    return high, mid, (rest - mid.astype(F32)).astype(BF16)


def product(a, b, dims):
    ah, am, al = a
    bh, bm, bl = b
    left = jnp.concatenate([ah, ah, am, ah, al, am], dims[0][0])
    right = jnp.concatenate([bh, bm, bh, bl, bh, bm], dims[1][0])
    return lax.dot_general(left, right, (dims, ((), ())), preferred_element_type=F32)


def nn(a, b):
    return product(a, b, ((1,), (0,)))


def nt(a, b):
    return product(a, b, ((1,), (1,)))


def tn(a, b):
    return product(a, b, ((0,), (0,)))


def block_rows(diagonal, rows):
    n, width = rows.shape
    groups = n // SUB
    tiles = width // S
    sub = lax.broadcasted_iota(jnp.int32, (SUB, S), 0)
    cols = [
        [
            jnp.broadcast_to(diagonal[SUB * g : SUB * (g + 1), j : j + 1], (SUB, S))
            if g >= j // SUB
            else None
            for g in range(groups)
        ]
        for j in range(n)
    ]
    work = [
        [rows[SUB * g : SUB * (g + 1), S * t : S * (t + 1)] for t in range(tiles)]
        for g in range(groups)
    ]
    scales = [jnp.zeros((SUB, S), F32)] * groups
    for k in range(n):
        gk, sk = divmod(k, SUB)
        scale = lax.rsqrt(jnp.broadcast_to(cols[k][gk][sk : sk + 1], (SUB, S)))
        factor = {g: cols[k][g] * scale for g in range(gk, groups)}
        scales[gk] = jnp.where(sub == sk, scale, scales[gk])
        for j in range(k + 1, n):
            gj, sj = divmod(j, SUB)
            other = factor[gj][sj : sj + 1]
            for g in range(gj, groups):
                cols[j][g] = cols[j][g] - factor[g] * other
        factor[gk] = jnp.where(sub > sk, factor[gk], 0.0)
        for t in range(tiles):
            pivot_row = work[gk][t][sk : sk + 1] * scale
            for g in range(gk + (sk == SUB - 1), groups):
                work[g][t] = work[g][t] - factor[g] * pivot_row
    return jnp.concatenate(
        [
            jnp.concatenate([tile * scales[g] for tile in work[g]], 1)
            for g in range(groups)
        ],
        0,
    )


def eliminate(whole):
    n = whole.shape[0]
    blocks = [whole[i : i + NB] for i in range(0, n, NB)]
    done = []
    for k in range(len(blocks)):
        upper = block_rows(blocks[k][:, k * NB : (k + 1) * NB], blocks[k])
        done.append(upper[:, n:])
        parts = split3(upper)
        for j in range(k + 1, len(blocks)):
            at = slice(j * NB, (j + 1) * NB)
            blocks[j] = blocks[j] - tn([p[:, at] for p in parts], parts)
    return jnp.concatenate(done, 0)


def squared_distances(cols, rows):
    dx = cols[:, 0:1] - rows[0:1]
    dy = cols[:, 1:2] - rows[1:2]
    return dx * dx + dy * dy


def pick(x, every):
    n, width = x.shape
    kept = width // every
    i = lax.broadcasted_iota(jnp.int32, (width, kept), 0)
    j = lax.broadcasted_iota(jnp.int32, (width, kept), 1)
    chosen = jnp.where(i == every * j, 1.0, 0.0).astype(BF16)
    parts = jnp.concatenate([p.astype(F32) for p in split3(x)], 0).astype(BF16)
    got = jnp.dot(parts, chosen, preferred_element_type=F32)
    return got[:n] + (got[n : 2 * n] + got[2 * n :])


def coupling(mine, other, scale):
    to_mine = jnp.log(squared_distances(mine.T, other)) * (other[2:3] * scale)
    to_other = jnp.log(squared_distances(other.T, mine)) * (mine[2:3] * scale)
    return to_mine, to_other


def prepare_kernel(
    rep_ref, coords_ref, density_ref, low_ref, high_ref,
    near_high_ref, near_mid_ref, far_ref, *rest,
):
    pair_refs, (wide, window, skeleton) = rest[:-3], rest[-3:]
    rep = rep_ref[0]
    width = coords_ref.shape[1]
    cells = width // LEAF
    wide[:, :LEAF] = low_ref[SUB:]
    wide[:2, LEAF : LEAF + width] = coords_ref[...]
    wide[2:3, LEAF : LEAF + width] = density_ref[...]
    wide[3:, LEAF : LEAF + width] = jnp.zeros((SUB - 3, width), F32)
    wide[:, LEAF + width :] = high_ref[SUB:]

    window[...] = wide[:, pl.ds(pl.multiple_of(rep * LEAF, LEAF), 3 * LEAF)]
    targets = window[:, LEAF : 2 * LEAF]

    def near_chunk(chunk, carry):
        at = pl.ds(pl.multiple_of(chunk * S, S), S)
        cols = window[:, at].T
        i = lax.broadcasted_iota(jnp.int32, (S, LEAF), 0) + (chunk * S - LEAF)
        same = i == lax.broadcasted_iota(jnp.int32, (S, LEAF), 1)
        squared = jnp.where(same, 1.0, squared_distances(cols, targets))
        itself = -2.0 * (1.0 - jnp.log(0.5 * cols[:, 2:3]))
        values = jnp.where(same, itself, jnp.log(squared)) * (cols[:, 2:3] * LOG_SCALE)
        high = values.astype(BF16)
        near_high_ref[at] = high
        near_mid_ref[at] = (values - high.astype(F32)).astype(BF16)
        return carry

    lax.fori_loop(0, 3 * LEAF // S, near_chunk, 0)

    leaves = [wide[:, LEAF * (i + 1) : LEAF * (i + 2)] for i in range(cells)]
    nodes = pick(jnp.concatenate(leaves, 0), STEP)
    for level, ref in enumerate(pair_refs):
        count = cells >> level
        for i in range(count):
            skeleton[i] = nodes[SUB * i : SUB * (i + 1)]
        index = rep >> level
        pair = coupling(
            skeleton[index], skeleton[index ^ 1], LOG_SCALE * (STEP << level)
        )
        for side in range(2):
            for part, value in enumerate(split3(pair[side])):
                ref[side, part] = value
        joined = [
            jnp.concatenate(
                [nodes[SUB * i : SUB * (i + 1)], nodes[SUB * (i + 1) : SUB * (i + 2)]], 1
            )
            for i in range(0, count, 2)
        ]
        nodes = pick(jnp.concatenate(joined, 0), 2)
    scale = jnp.where(
        lax.broadcasted_iota(jnp.int32, (SUB, S), 0) == 2,
        float(STEP << len(pair_refs)), 1.0,
    )
    far_ref[...] = nodes * scale


def leaf_kernel(data_ref, near_high_ref, near_mid_ref, z_ref, inverse_ref, hat_ref):
    near = jnp.zeros((S, LEAF), F32)
    for part in range(3):
        at = slice(part * LEAF, (part + 1) * LEAF)
        tests = data_ref[:, part + 1].reshape(S, LEAF)
        high, mid, _ = split3(tests)
        near_high, near_mid = near_high_ref[at], near_mid_ref[at]
        left = jnp.concatenate([high, high, mid], 1)
        right = jnp.concatenate([near_high, near_mid, near_high], 0)
        near = near + jnp.dot(left, right, preferred_element_type=F32)
    samples = data_ref[:, 0].reshape(S, LEAF)
    z = samples - near
    z_ref[...] = z
    parts = split3(z)
    both = [split3(samples), split3(data_ref[:, 2].reshape(S, LEAF))]
    gram = nt(parts, parts)
    rights = [nt(parts, x) for x in both]
    eye = jnp.where(
        lax.broadcasted_iota(jnp.int32, (S, S), 0) == lax.broadcasted_iota(jnp.int32, (S, S), 1),
        1.0, 0.0,
    ).astype(F32)
    got = eliminate(jnp.concatenate([gram, *rights, eye], 1))
    hat_ref[:S] = got[:, :S]
    hat_ref[S:] = got[:, S : 2 * S]
    inverse_ref[...] = got[:, 2 * S :]


def basis_kernel(inverse_ref, z_ref, q_ref):
    q = nn(split3(inverse_ref[...]), split3(z_ref[...])) * math.sqrt(LEAF)
    q_ref[...] = q.reshape(q_ref.shape)


def off_diagonal(to_mine, to_other, mine_ref, other_ref):
    z_mine = mine_ref[:S] - nn(to_mine, split3(other_ref[S : 2 * S]))
    z_other = other_ref[:S] - nn(to_other, split3(mine_ref[S : 2 * S]))
    return z_mine, z_other


def merge(to_mine, to_other, mine_ref, other_ref):
    z_mine, z_other = off_diagonal(to_mine, to_other, mine_ref, other_ref)
    left = split3(jnp.concatenate([z_mine.T, z_other.T], 1))
    mine = jnp.concatenate([z_mine, mine_ref[:S], mine_ref[S : 2 * S]], 1)
    other = jnp.concatenate([z_other, other_ref[:S], other_ref[S : 2 * S]], 1)
    return eliminate(nn(left, split3(jnp.concatenate([mine, other], 0))))


def near_parent_kernel(pair_ref, far_ref, mine_ref, other_ref, hat_ref):
    pair = [[pair_ref[side, part] for part in range(3)] for side in range(2)]
    got = merge(*pair, mine_ref, other_ref)
    hat_ref[:S] = got[:, :S]
    hat_ref[S : 2 * S] = got[:, S:]
    if hat_ref.shape[0] > 2 * S:
        hat_ref[2 * S :] = far_ref[...]


def far_parent_kernel(second_ref, mine_ref, other_ref, hat_ref):
    mine, other = mine_ref[2 * S :], other_ref[2 * S :]
    to_mine, to_other = coupling(mine, other, LOG_SCALE)
    got = merge(split3(to_mine), split3(to_other), mine_ref, other_ref)
    hat_ref[:S] = got[:, :S]
    hat_ref[S : 2 * S] = got[:, S:]
    second = second_ref[0] == 1
    joined = jnp.concatenate(
        [jnp.where(second, other, mine), jnp.where(second, mine, other)], 1
    )
    double = lax.broadcasted_iota(jnp.int32, (SUB, S), 0) == 2
    hat_ref[2 * S :] = pick(joined, 2) * jnp.where(double, 2.0, 1.0)


def top_kernel(place_ref, mine_ref, other_ref, q_ref, all_rows):
    mine, other = mine_ref[2 * S :], other_ref[2 * S :]
    to_mine, to_other = coupling(mine, other, LOG_SCALE)
    z_mine, z_other = off_diagonal(
        split3(to_mine), split3(to_other), mine_ref, other_ref
    )
    second = place_ref[0] == 1
    first = jnp.where(second, z_other, z_mine)
    last = jnp.where(second, z_mine, z_other)
    turned = jnp.concatenate([first.T, last.T], 1)
    gram = nn(split3(turned), split3(jnp.concatenate([first, last], 0)))
    all_rows[...] = eliminate(jnp.concatenate([gram, turned], 1)) * math.sqrt(2 * S)
    count = q_ref.shape[0]
    start = pl.multiple_of(place_ref[1] * count, count)
    q_ref[...] = all_rows[pl.ds(start, count)]


VMEM = pl.BlockSpec(memory_space=pltpu.VMEM)
SMEM = pl.BlockSpec(memory_space=pltpu.SMEM)


def call(kernel, outs, specs, *operands, scratch=(), flops=10**9):
    return pl.pallas_call(
        kernel,
        out_shape=[jax.ShapeDtypeStruct(shape, kind) for shape, kind in outs],
        in_specs=specs,
        out_specs=[VMEM] * len(outs),
        scratch_shapes=list(scratch),
        compiler_params=pltpu.CompilerParams(vmem_limit_bytes=32 * 1024 * 1024),
        cost_estimate=pl.CostEstimate(
            flops=flops, bytes_accessed=2**20, transcendentals=0
        ),
    )(*operands)


def swap(block, axis, mask):
    count = lax.axis_size(axis)
    return lax.ppermute(block, axis, [(i, i ^ mask) for i in range(count)])


def body(curve_coordinates, weighted_density, random_test_matrix, sketch_matrix):
    columns, width = random_test_matrix.shape
    cells = width // LEAF
    cell_levels = cells.bit_length() - 1
    rep = lax.axis_index("rep").astype(jnp.int32)
    leaf = lax.axis_index("leaf").astype(jnp.int32)
    count = lax.axis_size("leaf")

    density = weighted_density[None]

    def edge(at):
        return jnp.concatenate(
            [
                random_test_matrix[:, at],
                curve_coordinates[:, at],
                density[:, at],
                jnp.zeros((SUB - 3, LEAF), F32),
            ],
            0,
        )

    low = lax.ppermute(
        edge(slice(width - LEAF, width)), "leaf", [(i, (i + 1) % count) for i in range(count)]
    )
    high = lax.ppermute(
        edge(slice(0, LEAF)), "leaf", [(i, (i - 1) % count) for i in range(count)]
    )

    def by_leaf(block):
        return block.reshape(columns, -1, LEAF).transpose(1, 0, 2)

    tests = by_leaf(random_test_matrix)
    before = jnp.concatenate([low[None, :columns], tests[:-1]], 0)
    after = jnp.concatenate([tests[1:], high[None, :columns]], 0)
    parcels = jnp.stack([by_leaf(sketch_matrix), before, tests, after], 1)
    data = lax.all_to_all(parcels, "rep", 0, 0)

    near_high, near_mid, far, *pairs = call(
        prepare_kernel,
        [((3 * LEAF, LEAF), BF16)] * 2
        + [((SUB, S), F32)]
        + [((2, 3, S, S), BF16)] * cell_levels,
        [SMEM] + [VMEM] * 4,
        rep.reshape(1),
        curve_coordinates,
        density,
        low,
        high,
        scratch=[
            pltpu.VMEM((SUB, width + 2 * LEAF), F32),
            pltpu.VMEM((SUB, 3 * LEAF), F32),
            pltpu.VMEM((cells, SUB, S), F32),
        ],
        flops=10**10,
    )
    z, inverse, hat = call(
        leaf_kernel,
        [((S, LEAF), F32), ((S, S), F32), ((2 * S, S), F32)],
        [VMEM] * 3,
        data,
        near_high,
        near_mid,
    )
    (basis,) = call(
        basis_kernel, [((cells, columns, LEAF), F32)], [VMEM] * 2, inverse, z
    )
    leaf_basis = lax.all_to_all(basis, "rep", 0, 0)
    leaf_basis = leaf_basis.transpose(1, 0, 2).reshape(columns, width)

    for level, mask in enumerate((1, 3, 4, 12)):
        other = swap(hat, "rep", mask)
        rows = 2 * S + (SUB if level == cell_levels - 1 else 0)
        (hat,) = call(
            near_parent_kernel, [((rows, S), F32)], [VMEM] * 4, pairs[level], far, hat, other
        )
    for level, mask in enumerate((1, 2)):
        other = swap(hat, "leaf", mask)
        (hat,) = call(
            far_parent_kernel,
            [((2 * S + SUB, S), F32)],
            [SMEM] + [VMEM] * 2,
            (leaf >> level & 1).reshape(1),
            hat,
            other,
        )
    other = swap(hat, "leaf", 4)
    (top,) = call(
        top_kernel,
        [((columns, 2 * S), F32)],
        [SMEM] + [VMEM] * 2,
        jnp.stack([leaf >> 2 & 1, rep]),
        hat,
        other,
        scratch=[pltpu.VMEM((S, 2 * S), F32)],
    )
    return (leaf_basis, top[None])


def solution(mesh):
    return jax.shard_map(
        body,
        mesh=mesh,
        in_specs=(P(None, "leaf"), P("leaf"), P("rep", "leaf"), P("rep", "leaf")),
        out_specs=(P("rep", "leaf"), P("leaf", "rep", None)),
        check_vma=False,
    )
```

```python
import math

import jax
import jax.numpy as jnp
from jax import lax
from jax.experimental import pallas as pl
from jax.experimental.pallas import tpu as pltpu
from jax.sharding import PartitionSpec as P

LEAF = 512
S = 128
NB = 32
SUB = 8
STEP = LEAF // S
F32 = jnp.float32
BF16 = jnp.bfloat16
LOG_SCALE = -0.25 / math.pi
VMEM_LIMIT = 16 * 1024 * 1024


def split3(x):
    high = x.astype(BF16)
    rest = x - high.astype(F32)
    mid = rest.astype(BF16)
    return high, mid, (rest - mid.astype(F32)).astype(BF16)


def product(a, b, dims):
    ah, am, al = a
    bh, bm, bl = b
    left = jnp.concatenate([ah, ah, am, ah, al, am], dims[0][0])
    right = jnp.concatenate([bh, bm, bh, bl, bh, bm], dims[1][0])
    return lax.dot_general(left, right, (dims, ((), ())), preferred_element_type=F32)


def nn(a, b):
    return product(a, b, ((1,), (0,)))


def nt(a, b):
    return product(a, b, ((1,), (1,)))


def tn(a, b):
    return product(a, b, ((0,), (0,)))


def block_rows(diagonal, rows):
    n, width = rows.shape
    groups = n // SUB
    tiles = width // S
    sub = lax.broadcasted_iota(jnp.int32, (SUB, S), 0)
    cols = [
        [
            jnp.broadcast_to(diagonal[SUB * g : SUB * (g + 1), j : j + 1], (SUB, S))
            if g >= j // SUB
            else None
            for g in range(groups)
        ]
        for j in range(n)
    ]
    work = [
        [rows[SUB * g : SUB * (g + 1), S * t : S * (t + 1)] for t in range(tiles)]
        for g in range(groups)
    ]
    scales = [jnp.zeros((SUB, S), F32)] * groups
    for k in range(n):
        gk, sk = divmod(k, SUB)
        scale = lax.rsqrt(jnp.broadcast_to(cols[k][gk][sk : sk + 1], (SUB, S)))
        factor = {g: cols[k][g] * scale for g in range(gk, groups)}
        scales[gk] = jnp.where(sub == sk, scale, scales[gk])
        for j in range(k + 1, n):
            gj, sj = divmod(j, SUB)
            other = factor[gj][sj : sj + 1]
            for g in range(gj, groups):
                cols[j][g] = cols[j][g] - factor[g] * other
        factor[gk] = jnp.where(sub > sk, factor[gk], 0.0)
        for t in range(tiles):
            pivot_row = work[gk][t][sk : sk + 1] * scale
            for g in range(gk + (sk == SUB - 1), groups):
                work[g][t] = work[g][t] - factor[g] * pivot_row
    return jnp.concatenate(
        [
            jnp.concatenate([tile * scales[g] for tile in work[g]], 1)
            for g in range(groups)
        ],
        0,
    )


def eliminate(whole):
    n = whole.shape[0]
    blocks = [whole[i : i + NB] for i in range(0, n, NB)]
    done = []
    for k in range(len(blocks)):
        diagonal = blocks[k][:, k * NB : (k + 1) * NB]
        if k == len(blocks) - 1:
            done.append(block_rows(diagonal, blocks[k][:, n:]))
            break
        upper = block_rows(diagonal, blocks[k])
        done.append(upper[:, n:])
        parts = split3(upper)
        for j in range(k + 1, len(blocks)):
            at = slice(j * NB, (j + 1) * NB)
            blocks[j] = blocks[j] - tn([p[:, at] for p in parts], parts)
    return jnp.concatenate(done, 0)


def squared_distances(cols, rows):
    dx = cols[:, 0:1] - rows[0:1]
    dy = cols[:, 1:2] - rows[1:2]
    return dx * dx + dy * dy


def pick(x, every):
    n, width = x.shape
    kept = width // every
    i = lax.broadcasted_iota(jnp.int32, (width, kept), 0)
    j = lax.broadcasted_iota(jnp.int32, (width, kept), 1)
    chosen = jnp.where(i == every * j, 1.0, 0.0).astype(BF16)
    parts = jnp.concatenate([p.astype(F32) for p in split3(x)], 0).astype(BF16)
    got = jnp.dot(parts, chosen, preferred_element_type=F32)
    return got[:n] + (got[n : 2 * n] + got[2 * n :])


def coupling(mine, other, scale):
    to_mine = jnp.log(squared_distances(mine.T, other)) * (other[2:3] * scale)
    to_other = jnp.log(squared_distances(other.T, mine)) * (mine[2:3] * scale)
    return to_mine, to_other


def prepare_kernel(
    rep_ref, coords_ref, density_ref, low_ref, high_ref,
    near_high_ref, near_mid_ref, far_ref, *rest,
):
    pair_refs, (wide, window, skeleton) = rest[:-3], rest[-3:]
    rep = rep_ref[0]
    width = coords_ref.shape[1]
    cells = width // LEAF
    wide[:, :LEAF] = low_ref[SUB:]
    wide[:2, LEAF : LEAF + width] = coords_ref[...]
    wide[2:3, LEAF : LEAF + width] = density_ref[...]
    wide[3:, LEAF : LEAF + width] = jnp.zeros((SUB - 3, width), F32)
    wide[:, LEAF + width :] = high_ref[SUB:]

    window[...] = wide[:, pl.ds(pl.multiple_of(rep * LEAF, LEAF), 3 * LEAF)]
    targets = window[:, LEAF : 2 * LEAF]

    def near_chunk(chunk, carry):
        at = pl.ds(pl.multiple_of(chunk * S, S), S)
        cols = window[:, at].T
        i = lax.broadcasted_iota(jnp.int32, (S, LEAF), 0) + (chunk * S - LEAF)
        same = i == lax.broadcasted_iota(jnp.int32, (S, LEAF), 1)
        squared = jnp.where(same, 1.0, squared_distances(cols, targets))
        itself = -2.0 * (1.0 - jnp.log(0.5 * cols[:, 2:3]))
        values = jnp.where(same, itself, jnp.log(squared)) * (cols[:, 2:3] * LOG_SCALE)
        high = values.astype(BF16)
        near_high_ref[at] = high
        near_mid_ref[at] = (values - high.astype(F32)).astype(BF16)
        return carry

    lax.fori_loop(0, 3 * LEAF // S, near_chunk, 0)

    leaves = [wide[:, LEAF * (i + 1) : LEAF * (i + 2)] for i in range(cells)]
    nodes = pick(jnp.concatenate(leaves, 0), STEP)
    for level, ref in enumerate(pair_refs):
        count = cells >> level
        for i in range(count):
            skeleton[i] = nodes[SUB * i : SUB * (i + 1)]
        index = rep >> level
        pair = coupling(
            skeleton[index], skeleton[index ^ 1], LOG_SCALE * (STEP << level)
        )
        for side in range(2):
            for part, value in enumerate(split3(pair[side])):
                ref[side, part] = value
        joined = [
            jnp.concatenate(
                [nodes[SUB * i : SUB * (i + 1)], nodes[SUB * (i + 1) : SUB * (i + 2)]], 1
            )
            for i in range(0, count, 2)
        ]
        nodes = pick(jnp.concatenate(joined, 0), 2)
    scale = jnp.where(
        lax.broadcasted_iota(jnp.int32, (SUB, S), 0) == 2,
        float(STEP << len(pair_refs)), 1.0,
    )
    far_ref[...] = nodes * scale


def edges_kernel(
    first_ref, last_ref, first_coords_ref, last_coords_ref, density_ref, low_ref, high_ref
):
    width = density_ref.shape[1]
    sides = (
        (high_ref, first_ref, first_coords_ref, 0),
        (low_ref, last_ref, last_coords_ref, width - LEAF),
    )
    for ref, tests_ref, coords_ref, start in sides:
        ref[:SUB] = tests_ref[...]
        ref[SUB : SUB + 2] = coords_ref[...]
        ref[SUB + 2 : SUB + 3] = density_ref[:, start : start + LEAF]
        ref[SUB + 3 :] = jnp.zeros((SUB - 3, LEAF), F32)


def turn(index, turned):
    return jnp.where(turned == 1, index % 4 * 4 + index // 4, index)


def pack_kernel(turned_ref, samples_ref, tests_ref, low_ref, high_ref, out_ref, wide):
    width = samples_ref.shape[1]
    wide[:, :LEAF] = low_ref[:SUB]
    wide[:, LEAF : LEAF + width] = tests_ref[...]
    wide[:, LEAF + width :] = high_ref[:SUB]
    for i in range(out_ref.shape[0]):
        leaf = turn(jnp.int32(i), turned_ref[0])
        out_ref[i, 0] = samples_ref[:, pl.ds(pl.multiple_of(leaf * LEAF, LEAF), LEAF)]
        for side in range(3):
            start = pl.multiple_of((leaf + side) * LEAF, LEAF)
            out_ref[i, side + 1] = wide[:, pl.ds(start, LEAF)]


def leaf_kernel(
    data_ref, near_high_ref, near_mid_hbm, z_ref, inverse_ref, hat_ref, near_mid_ref, sem
):
    fetch = pltpu.make_async_copy(near_mid_hbm, near_mid_ref, sem)
    fetch.start()
    near = jnp.zeros((S, LEAF), F32)
    highs = []
    for part in range(3):
        near_high = near_high_ref[part * LEAF : (part + 1) * LEAF]
        high, mid, _ = split3(data_ref[:, part + 1].reshape(S, LEAF))
        left = jnp.concatenate([high, mid], 1)
        right = jnp.concatenate([near_high, near_high], 0)
        near = near + jnp.dot(left, right, preferred_element_type=F32)
        highs.append(high)
    fetch.wait()
    near = near + jnp.dot(
        jnp.concatenate(highs, 1), near_mid_ref[...], preferred_element_type=F32
    )
    samples = data_ref[:, 0].reshape(S, LEAF)
    z = samples - near
    z_ref[...] = z
    parts = split3(z)
    both = [split3(samples), split3(data_ref[:, 2].reshape(S, LEAF))]
    gram = nt(parts, parts)
    rights = [nt(parts, x) for x in both]
    eye = jnp.where(
        lax.broadcasted_iota(jnp.int32, (S, S), 0) == lax.broadcasted_iota(jnp.int32, (S, S), 1),
        1.0, 0.0,
    ).astype(F32)
    got = eliminate(jnp.concatenate([gram, *rights, eye], 1))
    hat_ref[:S] = got[:, :S]
    hat_ref[S:] = got[:, S : 2 * S]
    inverse_ref[...] = got[:, 2 * S :]


def basis_kernel(inverse_ref, z_ref, q_ref):
    q = nn(split3(inverse_ref[...]), split3(z_ref[...])) * math.sqrt(LEAF)
    q_ref[...] = q.reshape(q_ref.shape)


def off_diagonal(to_mine, to_other, mine_ref, other_ref):
    z_mine = mine_ref[:S] - nn(to_mine, split3(other_ref[S : 2 * S]))
    z_other = other_ref[:S] - nn(to_other, split3(mine_ref[S : 2 * S]))
    return z_mine, z_other


def merge(to_mine, to_other, mine_ref, other_ref):
    z_mine, z_other = off_diagonal(to_mine, to_other, mine_ref, other_ref)
    left = split3(jnp.concatenate([z_mine.T, z_other.T], 1))
    mine = jnp.concatenate([z_mine, mine_ref[:S], mine_ref[S : 2 * S]], 1)
    other = jnp.concatenate([z_other, other_ref[:S], other_ref[S : 2 * S]], 1)
    return eliminate(nn(left, split3(jnp.concatenate([mine, other], 0))))


def near_parent_kernel(pair_ref, far_ref, mine_ref, other_ref, hat_ref):
    pair = [[pair_ref[side, part] for part in range(3)] for side in range(2)]
    got = merge(*pair, mine_ref, other_ref)
    hat_ref[:S] = got[:, :S]
    hat_ref[S : 2 * S] = got[:, S:]
    if hat_ref.shape[0] > 2 * S:
        hat_ref[2 * S :] = far_ref[...]


def far_parent_kernel(second_ref, mine_ref, other_ref, hat_ref, *half_refs):
    mine, other = mine_ref[2 * S :], other_ref[2 * S :]
    to_mine, to_other = coupling(mine, other, LOG_SCALE)
    got = merge(split3(to_mine), split3(to_other), mine_ref, other_ref)
    hat_ref[:S] = got[:, :S]
    hat_ref[S : 2 * S] = got[:, S:]
    second = second_ref[0] == 1
    joined = jnp.concatenate(
        [jnp.where(second, other, mine), jnp.where(second, mine, other)], 1
    )
    double = lax.broadcasted_iota(jnp.int32, (SUB, S), 0) == 2
    hat_ref[2 * S :] = pick(joined, 2) * jnp.where(double, 2.0, 1.0)
    for half_ref in half_refs:
        half_ref[...] = jnp.where(second_ref[1] == 1, hat_ref[S:], hat_ref[: S + SUB])


def top_kernel(
    place_ref, mine_ref, direct_ref, passed_ref, parts_ref, q_ref, basis_ref,
    all_rows, other_ref, sems,
):
    copies = []
    for i in range(parts_ref.shape[0]):
        leaf = turn(jnp.int32(i), place_ref[2])
        to = basis_ref.at[:, pl.ds(pl.multiple_of(leaf * LEAF, LEAF), LEAF)]
        copies.append(pltpu.make_async_copy(parts_ref.at[i], to, sems.at[i]))
        copies[-1].start()
    upper_direct = place_ref[2] == 0
    other_ref[: S + SUB] = jnp.where(upper_direct, direct_ref[...], passed_ref[...])
    other_ref[S:] = jnp.where(upper_direct, passed_ref[...], direct_ref[...])
    mine, other = mine_ref[2 * S :], other_ref[2 * S :]
    to_mine, to_other = coupling(mine, other, LOG_SCALE)
    z_mine, z_other = off_diagonal(
        split3(to_mine), split3(to_other), mine_ref, other_ref
    )
    second = place_ref[0] == 1
    first = jnp.where(second, z_other, z_mine)
    last = jnp.where(second, z_mine, z_other)
    turned = jnp.concatenate([first.T, last.T], 1)
    gram = nn(split3(turned), split3(jnp.concatenate([first, last], 0)))
    all_rows[...] = eliminate(jnp.concatenate([gram, turned], 1)) * math.sqrt(2 * S)
    count = q_ref.shape[0]
    start = pl.multiple_of(place_ref[1] * count, count)
    q_ref[...] = all_rows[pl.ds(start, count)]
    for copy in copies:
        copy.wait()


VMEM = pl.BlockSpec(memory_space=pltpu.VMEM)
SMEM = pl.BlockSpec(memory_space=pltpu.SMEM)
ANY = pl.BlockSpec(memory_space=pl.ANY)


def call(kernel, outs, specs, *operands, out_specs=None, scratch=(), flops=10**9):
    return pl.pallas_call(
        kernel,
        out_shape=[jax.ShapeDtypeStruct(shape, kind) for shape, kind in outs],
        in_specs=specs,
        out_specs=out_specs or [VMEM] * len(outs),
        scratch_shapes=list(scratch),
        compiler_params=pltpu.CompilerParams(vmem_limit_bytes=VMEM_LIMIT),
        cost_estimate=pl.CostEstimate(
            flops=flops, bytes_accessed=2**20, transcendentals=0
        ),
    )(*operands)


def swap(block, even, odd):
    leaves, reps = lax.axis_size("leaf"), lax.axis_size("rep")
    route = [
        (i * reps + j, i * reps + (j ^ (odd if i % 2 else even)))
        for i in range(leaves)
        for j in range(reps)
    ]
    return lax.ppermute(block, ("leaf", "rep"), route)


def cross(block, mask):
    count = lax.axis_size("leaf")
    return lax.ppermute(block, "leaf", [(i, i ^ mask) for i in range(count)])


def body(curve_coordinates, weighted_density, random_test_matrix, sketch_matrix):
    columns, width = random_test_matrix.shape
    cells = width // LEAF
    cell_levels = cells.bit_length() - 1
    rep = lax.axis_index("rep").astype(jnp.int32)
    leaf = lax.axis_index("leaf").astype(jnp.int32)
    count = lax.axis_size("leaf")
    turned = leaf & 1
    own = turn(rep, turned)

    density = weighted_density[None]

    def edge(rows, last):
        return pl.BlockSpec((rows, LEAF), lambda i: (0, cells - 1 if last else 0))

    low, high = pl.pallas_call(
        edges_kernel,
        grid=(1,),
        out_shape=[jax.ShapeDtypeStruct((2 * SUB, LEAF), F32)] * 2,
        in_specs=[edge(columns, False), edge(columns, True), edge(2, False), edge(2, True)]
        + [pl.BlockSpec((1, width), lambda i: (0, 0))],
        out_specs=[pl.BlockSpec((2 * SUB, LEAF), lambda i: (0, 0))] * 2,
    )(random_test_matrix, random_test_matrix, curve_coordinates, curve_coordinates, density)
    low = lax.ppermute(low, "leaf", [(i, (i + 1) % count) for i in range(count)])
    high = lax.ppermute(high, "leaf", [(i, (i - 1) % count) for i in range(count)])

    (parcels,) = call(
        pack_kernel,
        [((cells, 4, columns, LEAF), F32)],
        [SMEM] + [VMEM] * 4,
        turned.reshape(1),
        sketch_matrix,
        random_test_matrix,
        low,
        high,
        scratch=[pltpu.VMEM((columns, width + 2 * LEAF), F32)],
    )
    data = lax.all_to_all(parcels, "rep", 0, 0)

    near_high, near_mid, far, *pairs = call(
        prepare_kernel,
        [((3 * LEAF, LEAF), BF16)] * 2
        + [((SUB, S), F32)]
        + [((2, 3, S, S), BF16)] * cell_levels,
        [SMEM] + [VMEM] * 4,
        own.reshape(1),
        curve_coordinates,
        density,
        low,
        high,
        scratch=[
            pltpu.VMEM((SUB, width + 2 * LEAF), F32),
            pltpu.VMEM((SUB, 3 * LEAF), F32),
            pltpu.VMEM((cells, SUB, S), F32),
        ],
        flops=10**10,
    )
    z, inverse, hat = call(
        leaf_kernel,
        [((S, LEAF), F32), ((S, S), F32), ((2 * S, S), F32)],
        [VMEM, VMEM, ANY],
        data,
        near_high,
        near_mid,
        scratch=[pltpu.VMEM((3 * LEAF, LEAF), BF16), pltpu.SemaphoreType.DMA],
    )
    (basis,) = call(
        basis_kernel, [((cells, columns, LEAF), F32)], [VMEM] * 2, inverse, z
    )
    parts = lax.all_to_all(basis, "rep", 0, 0)

    for level, masks in enumerate(((1, 4), (3, 12), (4, 1), (12, 3))):
        other = swap(hat, *masks)
        rows = 2 * S + (SUB if level == cell_levels - 1 else 0)
        (hat,) = call(
            near_parent_kernel, [((rows, S), F32)], [VMEM] * 4, pairs[level], far, hat, other
        )
    for level in range(2):
        other = cross(hat, 1 << level)
        hat, *half = call(
            far_parent_kernel,
            [((2 * S + SUB, S), F32), ((S + SUB, S), F32)][: level + 1],
            [SMEM] + [VMEM] * 2,
            jnp.stack([leaf >> level & 1, turned]),
            hat,
            other,
        )
    direct = cross(half[0], 4)
    top, leaf_basis = call(
        top_kernel,
        [((columns, 2 * S), F32), ((columns, width), F32)],
        [SMEM] + [VMEM] * 3 + [ANY],
        jnp.stack([leaf >> 2 & 1, rep, turned]),
        hat,
        direct,
        cross(direct, 1),
        parts,
        out_specs=[VMEM, ANY],
        scratch=[
            pltpu.VMEM((S, 2 * S), F32),
            pltpu.VMEM((2 * S + SUB, S), F32),
            pltpu.SemaphoreType.DMA((cells,)),
        ],
    )
    return (leaf_basis, top[None])


def solution(mesh):
    return jax.shard_map(
        body,
        mesh=mesh,
        in_specs=(P(None, "leaf"), P("leaf"), P("rep", "leaf"), P("rep", "leaf")),
        out_specs=(P("rep", "leaf"), P("leaf", "rep", None)),
        check_vma=False,
    )
```

```python
import math

import jax
import jax.numpy as jnp
from jax import lax
from jax.experimental import pallas as pl
from jax.experimental.pallas import tpu as pltpu
from jax.sharding import PartitionSpec as P

LEAF = 512
S = 128
NB = 32
SUB = 8
STEP = LEAF // S
F32 = jnp.float32
BF16 = jnp.bfloat16
LOG_SCALE = -0.25 / math.pi
VMEM_LIMIT = 16 * 1024 * 1024


def split3(x):
    high = x.astype(BF16)
    rest = x - high.astype(F32)
    mid = rest.astype(BF16)
    return high, mid, (rest - mid.astype(F32)).astype(BF16)


def product(a, b, dims):
    ah, am, al = a
    bh, bm, bl = b
    left = jnp.concatenate([ah, ah, am, ah, al, am], dims[0][0])
    right = jnp.concatenate([bh, bm, bh, bl, bh, bm], dims[1][0])
    return lax.dot_general(left, right, (dims, ((), ())), preferred_element_type=F32)


def nn(a, b):
    return product(a, b, ((1,), (0,)))


def nt(a, b):
    return product(a, b, ((1,), (1,)))


def tn(a, b):
    return product(a, b, ((0,), (0,)))


def block_rows(diagonal, rows):
    n, width = rows.shape
    groups = n // SUB
    tiles = width // S
    sub = lax.broadcasted_iota(jnp.int32, (SUB, S), 0)
    cols = [
        [
            jnp.broadcast_to(diagonal[SUB * g : SUB * (g + 1), j : j + 1], (SUB, S))
            if g >= j // SUB
            else None
            for g in range(groups)
        ]
        for j in range(n)
    ]
    work = [
        [rows[SUB * g : SUB * (g + 1), S * t : S * (t + 1)] for t in range(tiles)]
        for g in range(groups)
    ]
    scales = [jnp.zeros((SUB, S), F32)] * groups
    factors = []

    def update(j, k):
        gj, sj = divmod(j, SUB)
        other = factors[k][gj][sj : sj + 1]
        for g in range(gj, groups):
            cols[j][g] = cols[j][g] - factors[k][g] * other

    for k in range(n):
        gk, sk = divmod(k, SUB)
        scale = lax.rsqrt(jnp.broadcast_to(cols[k][gk][sk : sk + 1], (SUB, S)))
        factor = {g: cols[k][g] * scale for g in range(gk, groups)}
        factors.append(dict(factor))
        scales[gk] = jnp.where(sub == sk, scale, scales[gk])
        if k + 1 < n:
            update(k + 1, k)
        if k + 2 < n:
            for earlier in range(k + 1):
                update(k + 2, earlier)
        factor[gk] = jnp.where(sub > sk, factor[gk], 0.0)
        for t in range(tiles):
            pivot_row = work[gk][t][sk : sk + 1] * scale
            for g in range(gk + (sk == SUB - 1), groups):
                work[g][t] = work[g][t] - factor[g] * pivot_row
    return jnp.concatenate(
        [
            jnp.concatenate([tile * scales[g] for tile in work[g]], 1)
            for g in range(groups)
        ],
        0,
    )


def eliminate(whole):
    n = whole.shape[0]
    blocks = [whole[i : i + NB] for i in range(0, n, NB)]
    done = []
    for k in range(len(blocks)):
        diagonal = blocks[k][:, k * NB : (k + 1) * NB]
        if k == len(blocks) - 1:
            done.append(block_rows(diagonal, blocks[k][:, n:]))
            break
        upper = block_rows(diagonal, blocks[k])
        done.append(upper[:, n:])
        parts = split3(upper)
        for j in range(k + 1, len(blocks)):
            at = slice(j * NB, (j + 1) * NB)
            blocks[j] = blocks[j] - tn([p[:, at] for p in parts], parts)
    return jnp.concatenate(done, 0)


def squared_distances(cols, rows):
    dx = cols[:, 0:1] - rows[0:1]
    dy = cols[:, 1:2] - rows[1:2]
    return dx * dx + dy * dy


def pick(x, every):
    n, width = x.shape
    kept = width // every
    i = lax.broadcasted_iota(jnp.int32, (width, kept), 0)
    j = lax.broadcasted_iota(jnp.int32, (width, kept), 1)
    chosen = jnp.where(i == every * j, 1.0, 0.0).astype(BF16)
    parts = jnp.concatenate([p.astype(F32) for p in split3(x)], 0).astype(BF16)
    got = jnp.dot(parts, chosen, preferred_element_type=F32)
    return got[:n] + (got[n : 2 * n] + got[2 * n :])


def coupling(mine, other, scale):
    to_mine = jnp.log(squared_distances(mine.T, other)) * (other[2:3] * scale)
    to_other = jnp.log(squared_distances(other.T, mine)) * (mine[2:3] * scale)
    return to_mine, to_other


def prepare_kernel(
    rep_ref, coords_ref, density_ref, low_ref, high_ref,
    near_high_ref, near_mid_hbm, far_ref, *rest,
):
    pair_refs, (wide, window, skeleton, near_mid_ref, sem) = rest[:-5], rest[-5:]
    rep = rep_ref[0]
    width = coords_ref.shape[1]
    cells = width // LEAF
    wide[:, :LEAF] = low_ref[SUB:]
    wide[:2, LEAF : LEAF + width] = coords_ref[...]
    wide[2:3, LEAF : LEAF + width] = density_ref[...]
    wide[3:, LEAF : LEAF + width] = jnp.zeros((SUB - 3, width), F32)
    wide[:, LEAF + width :] = high_ref[SUB:]

    window[...] = wide[:, pl.ds(pl.multiple_of(rep * LEAF, LEAF), 3 * LEAF)]
    targets = window[:, LEAF : 2 * LEAF]

    def near_chunk(chunk, carry):
        at = pl.ds(pl.multiple_of(chunk * S, S), S)
        cols = window[:, at].T
        i = lax.broadcasted_iota(jnp.int32, (S, LEAF), 0) + (chunk * S - LEAF)
        same = i == lax.broadcasted_iota(jnp.int32, (S, LEAF), 1)
        squared = jnp.where(same, 1.0, squared_distances(cols, targets))
        itself = -2.0 * (1.0 - jnp.log(0.5 * cols[:, 2:3]))
        values = jnp.where(same, itself, jnp.log(squared)) * (cols[:, 2:3] * LOG_SCALE)
        high = values.astype(BF16)
        near_high_ref[at] = high
        near_mid_ref[at] = (values - high.astype(F32)).astype(BF16)
        return carry

    lax.fori_loop(0, 3 * LEAF // S, near_chunk, 0)
    store = pltpu.make_async_copy(near_mid_ref, near_mid_hbm, sem)
    store.start()

    leaves = [wide[:, LEAF * (i + 1) : LEAF * (i + 2)] for i in range(cells)]
    nodes = pick(jnp.concatenate(leaves, 0), STEP)
    for level, ref in enumerate(pair_refs):
        count = cells >> level
        for i in range(count):
            skeleton[i] = nodes[SUB * i : SUB * (i + 1)]
        index = rep >> level
        pair = coupling(
            skeleton[index], skeleton[index ^ 1], LOG_SCALE * (STEP << level)
        )
        for side in range(2):
            for part, value in enumerate(split3(pair[side])):
                ref[side, part] = value
        joined = [
            jnp.concatenate(
                [nodes[SUB * i : SUB * (i + 1)], nodes[SUB * (i + 1) : SUB * (i + 2)]], 1
            )
            for i in range(0, count, 2)
        ]
        nodes = pick(jnp.concatenate(joined, 0), 2)
    scale = jnp.where(
        lax.broadcasted_iota(jnp.int32, (SUB, S), 0) == 2,
        float(STEP << len(pair_refs)), 1.0,
    )
    far_ref[...] = nodes * scale
    store.wait()


def edges_kernel(
    first_ref, last_ref, first_coords_ref, last_coords_ref, density_ref, low_ref, high_ref
):
    width = density_ref.shape[1]
    sides = (
        (high_ref, first_ref, first_coords_ref, 0),
        (low_ref, last_ref, last_coords_ref, width - LEAF),
    )
    for ref, tests_ref, coords_ref, start in sides:
        ref[:SUB] = tests_ref[...]
        ref[SUB : SUB + 2] = coords_ref[...]
        ref[SUB + 2 : SUB + 3] = density_ref[:, start : start + LEAF]
        ref[SUB + 3 :] = jnp.zeros((SUB - 3, LEAF), F32)


def turn(index, turned):
    return jnp.where(turned == 1, index % 4 * 4 + index // 4, index)


def pack_kernel(turned_ref, samples_ref, tests_ref, out_ref, sems):
    cells = out_ref.shape[0]
    copies = []

    def move(source, leaf, i, slot):
        start = pl.multiple_of(leaf * LEAF, LEAF)
        copies.append(
            pltpu.make_async_copy(
                source.at[:, pl.ds(start, LEAF)], out_ref.at[i, slot], sems.at[len(copies)]
            )
        )
        copies[-1].start()

    for i in range(cells):
        leaf = turn(jnp.int32(i), turned_ref[0])
        move(samples_ref, leaf, i, 0)
        if i > 0:
            move(tests_ref, leaf - 1, i, 1)
        move(tests_ref, leaf, i, 2)
        if i < cells - 1:
            move(tests_ref, leaf + 1, i, 3)
    for copy in copies:
        copy.wait()


def ends_kernel(packed_ref, low_ref, high_ref, out_ref, sems):
    copies = [
        pltpu.make_async_copy(low_ref.at[:SUB], out_ref.at[0, 1], sems.at[0]),
        pltpu.make_async_copy(
            high_ref.at[:SUB], out_ref.at[out_ref.shape[0] - 1, 3], sems.at[1]
        ),
    ]
    for copy in copies:
        copy.start()
    for copy in copies:
        copy.wait()


def leaf_kernel(
    data_ref, near_high_ref, near_mid_hbm, z_ref, inverse_ref, hat_ref, near_mid_ref, sem
):
    fetch = pltpu.make_async_copy(near_mid_hbm, near_mid_ref, sem)
    fetch.start()
    near = jnp.zeros((S, LEAF), F32)
    highs = []
    for part in range(3):
        near_high = near_high_ref[part * LEAF : (part + 1) * LEAF]
        high, mid, _ = split3(data_ref[:, part + 1].reshape(S, LEAF))
        left = jnp.concatenate([high, mid], 1)
        right = jnp.concatenate([near_high, near_high], 0)
        near = near + jnp.dot(left, right, preferred_element_type=F32)
        highs.append(high)
    fetch.wait()
    near = near + jnp.dot(
        jnp.concatenate(highs, 1), near_mid_ref[...], preferred_element_type=F32
    )
    samples = data_ref[:, 0].reshape(S, LEAF)
    z = samples - near
    z_ref[...] = z
    parts = split3(z)
    both = [split3(samples), split3(data_ref[:, 2].reshape(S, LEAF))]
    gram = nt(parts, parts)
    rights = [nt(parts, x) for x in both]
    eye = jnp.where(
        lax.broadcasted_iota(jnp.int32, (S, S), 0) == lax.broadcasted_iota(jnp.int32, (S, S), 1),
        1.0, 0.0,
    ).astype(F32)
    got = eliminate(jnp.concatenate([gram, *rights, eye], 1))
    hat_ref[:S] = got[:, :S]
    hat_ref[S:] = got[:, S : 2 * S]
    inverse_ref[...] = got[:, 2 * S :]


def basis_kernel(inverse_ref, z_ref, q_ref):
    q = nn(split3(inverse_ref[...]), split3(z_ref[...])) * math.sqrt(LEAF)
    q_ref[...] = q.reshape(q_ref.shape)


def off_diagonal(to_mine, to_other, mine_ref, other_ref):
    z_mine = mine_ref[:S] - nn(to_mine, split3(other_ref[S : 2 * S]))
    z_other = other_ref[:S] - nn(to_other, split3(mine_ref[S : 2 * S]))
    return z_mine, z_other


def merge(to_mine, to_other, mine_ref, other_ref):
    z_mine, z_other = off_diagonal(to_mine, to_other, mine_ref, other_ref)
    left = split3(jnp.concatenate([z_mine.T, z_other.T], 1))
    mine = jnp.concatenate([z_mine, mine_ref[:S], mine_ref[S : 2 * S]], 1)
    other = jnp.concatenate([z_other, other_ref[:S], other_ref[S : 2 * S]], 1)
    return eliminate(nn(left, split3(jnp.concatenate([mine, other], 0))))


def far_kernel(second_ref, mine_ref, other_ref, pair_ref, *joined_refs):
    mine, other = mine_ref[...], other_ref[...]
    for side, block in enumerate(coupling(mine, other, LOG_SCALE)):
        for part, value in enumerate(split3(block)):
            pair_ref[side, part] = value
    second = second_ref[0] == 1
    joined = jnp.concatenate(
        [jnp.where(second, other, mine), jnp.where(second, mine, other)], 1
    )
    double = lax.broadcasted_iota(jnp.int32, (SUB, S), 0) == 2
    for ref in joined_refs:
        ref[...] = pick(joined, 2) * jnp.where(double, 2.0, 1.0)


def parent_kernel(pair_ref, mine_ref, other_ref, hat_ref):
    pair = [[pair_ref[side, part] for part in range(3)] for side in range(2)]
    got = merge(*pair, mine_ref, other_ref)
    hat_ref[:S] = got[:, :S]
    hat_ref[S:] = got[:, S:]


def last_parent_kernel(turned_ref, pair_ref, mine_ref, other_ref, hat_ref, half_ref):
    parent_kernel(pair_ref, mine_ref, other_ref, hat_ref)
    half_ref[...] = jnp.where(turned_ref[0] == 1, hat_ref[S:], hat_ref[:S])


def top_kernel(
    place_ref, pair_ref, mine_ref, direct_ref, passed_ref, parts_ref, q_ref, basis_ref,
    all_rows, other_ref, sems,
):
    copies = []
    for i in range(parts_ref.shape[0]):
        leaf = turn(jnp.int32(i), place_ref[2])
        to = basis_ref.at[:, pl.ds(pl.multiple_of(leaf * LEAF, LEAF), LEAF)]
        copies.append(pltpu.make_async_copy(parts_ref.at[i], to, sems.at[i]))
        copies[-1].start()
    upper_direct = place_ref[2] == 0
    other_ref[:S] = jnp.where(upper_direct, direct_ref[...], passed_ref[...])
    other_ref[S:] = jnp.where(upper_direct, passed_ref[...], direct_ref[...])
    pair = [[pair_ref[side, part] for part in range(3)] for side in range(2)]
    z_mine, z_other = off_diagonal(*pair, mine_ref, other_ref)
    second = place_ref[0] == 1
    first = jnp.where(second, z_other, z_mine)
    last = jnp.where(second, z_mine, z_other)
    turned = jnp.concatenate([first.T, last.T], 1)
    gram = nn(split3(turned), split3(jnp.concatenate([first, last], 0)))
    all_rows[...] = eliminate(jnp.concatenate([gram, turned], 1)) * math.sqrt(2 * S)
    count = q_ref.shape[0]
    start = pl.multiple_of(place_ref[1] * count, count)
    q_ref[...] = all_rows[pl.ds(start, count)]
    for copy in copies:
        copy.wait()


VMEM = pl.BlockSpec(memory_space=pltpu.VMEM)
SMEM = pl.BlockSpec(memory_space=pltpu.SMEM)
ANY = pl.BlockSpec(memory_space=pl.ANY)
HBM = pl.BlockSpec(memory_space=pltpu.HBM)


def call(kernel, outs, specs, *operands, out_specs=None, scratch=(), aliases={}, flops=10**9):
    return pl.pallas_call(
        kernel,
        out_shape=[jax.ShapeDtypeStruct(shape, kind) for shape, kind in outs],
        in_specs=specs,
        out_specs=out_specs or [VMEM] * len(outs),
        scratch_shapes=list(scratch),
        input_output_aliases=aliases,
        compiler_params=pltpu.CompilerParams(vmem_limit_bytes=VMEM_LIMIT),
        cost_estimate=pl.CostEstimate(
            flops=flops, bytes_accessed=2**20, transcendentals=0
        ),
    )(*operands)


def swap(block, even, odd):
    leaves, reps = lax.axis_size("leaf"), lax.axis_size("rep")
    route = [
        (i * reps + j, i * reps + (j ^ (odd if i % 2 else even)))
        for i in range(leaves)
        for j in range(reps)
    ]
    return lax.ppermute(block, ("leaf", "rep"), route)


def cross(block, mask):
    count = lax.axis_size("leaf")
    return lax.ppermute(block, "leaf", [(i, i ^ mask) for i in range(count)])


def body(curve_coordinates, weighted_density, random_test_matrix, sketch_matrix):
    columns, width = random_test_matrix.shape
    cells = width // LEAF
    cell_levels = cells.bit_length() - 1
    rep = lax.axis_index("rep").astype(jnp.int32)
    leaf = lax.axis_index("leaf").astype(jnp.int32)
    count = lax.axis_size("leaf")
    turned = leaf & 1
    own = turn(rep, turned)

    density = weighted_density[None]

    def edge(rows, last):
        return pl.BlockSpec((rows, LEAF), lambda i: (0, cells - 1 if last else 0))

    low, high = pl.pallas_call(
        edges_kernel,
        grid=(1,),
        out_shape=[jax.ShapeDtypeStruct((2 * SUB, LEAF), F32)] * 2,
        in_specs=[edge(columns, False), edge(columns, True), edge(2, False), edge(2, True)]
        + [pl.BlockSpec((1, width), lambda i: (0, 0))],
        out_specs=[pl.BlockSpec((2 * SUB, LEAF), lambda i: (0, 0))] * 2,
    )(random_test_matrix, random_test_matrix, curve_coordinates, curve_coordinates, density)
    low = lax.ppermute(low, "leaf", [(i, (i + 1) % count) for i in range(count)])
    high = lax.ppermute(high, "leaf", [(i, (i - 1) % count) for i in range(count)])

    (parcels,) = call(
        pack_kernel,
        [((cells, 4, columns, LEAF), F32)],
        [SMEM, HBM, HBM],
        turned.reshape(1),
        sketch_matrix,
        random_test_matrix,
        out_specs=[HBM],
        scratch=[pltpu.SemaphoreType.DMA((4 * cells - 2,))],
    )
    (parcels,) = call(
        ends_kernel,
        [((cells, 4, columns, LEAF), F32)],
        [HBM, HBM, HBM],
        parcels,
        low,
        high,
        out_specs=[HBM],
        scratch=[pltpu.SemaphoreType.DMA((2,))],
        aliases={0: 0},
        flops=10**6,
    )
    data = lax.all_to_all(parcels, "rep", 0, 0)

    near_high, near_mid, far, *pairs = call(
        prepare_kernel,
        [((3 * LEAF, LEAF), BF16)] * 2
        + [((SUB, S), F32)]
        + [((2, 3, S, S), BF16)] * cell_levels,
        [SMEM] + [VMEM] * 4,
        own.reshape(1),
        curve_coordinates,
        density,
        low,
        high,
        scratch=[
            pltpu.VMEM((SUB, width + 2 * LEAF), F32),
            pltpu.VMEM((SUB, 3 * LEAF), F32),
            pltpu.VMEM((cells, SUB, S), F32),
            pltpu.VMEM((3 * LEAF, LEAF), BF16),
            pltpu.SemaphoreType.DMA,
        ],
        out_specs=[VMEM, HBM] + [VMEM] * (cell_levels + 1),
        flops=10**10,
    )
    z, inverse, hat = call(
        leaf_kernel,
        [((S, LEAF), F32), ((S, S), F32), ((2 * S, S), F32)],
        [VMEM, VMEM, HBM],
        data,
        near_high,
        near_mid,
        scratch=[pltpu.VMEM((3 * LEAF, LEAF), BF16), pltpu.SemaphoreType.DMA],
    )
    (basis,) = call(
        basis_kernel, [((cells, columns, LEAF), F32)], [VMEM] * 2, inverse, z
    )
    parts = lax.all_to_all(basis, "rep", 0, 0)

    skeleton = far
    for level in range(3):
        pair, *joined = call(
            far_kernel,
            [((2, 3, S, S), BF16), ((SUB, S), F32)][: 2 - level // 2],
            [SMEM] + [VMEM] * 2,
            (leaf >> level & 1).reshape(1),
            skeleton,
            cross(skeleton, 1 << level),
        )
        pairs.append(pair)
        skeleton = joined[0] if joined else None

    for pair, masks in zip(pairs, ((1, 4), (3, 12), (4, 1), (12, 3))):
        (hat,) = call(
            parent_kernel, [((2 * S, S), F32)], [VMEM] * 3, pair, hat, swap(hat, *masks)
        )
    (hat,) = call(
        parent_kernel, [((2 * S, S), F32)], [VMEM] * 3, pairs[-3], hat, cross(hat, 1)
    )
    hat, half = call(
        last_parent_kernel,
        [((2 * S, S), F32), ((S, S), F32)],
        [SMEM] + [VMEM] * 3,
        turned.reshape(1),
        pairs[-2],
        hat,
        cross(hat, 2),
    )
    direct = cross(half, 4)
    top, leaf_basis = call(
        top_kernel,
        [((columns, 2 * S), F32), ((columns, width), F32)],
        [SMEM] + [VMEM] * 4 + [ANY],
        jnp.stack([leaf >> 2 & 1, rep, turned]),
        pairs[-1],
        hat,
        direct,
        cross(direct, 1),
        parts,
        out_specs=[VMEM, ANY],
        scratch=[
            pltpu.VMEM((S, 2 * S), F32),
            pltpu.VMEM((2 * S, S), F32),
            pltpu.SemaphoreType.DMA((cells,)),
        ],
    )
    return (leaf_basis, top[None])


def solution(mesh):
    return jax.shard_map(
        body,
        mesh=mesh,
        in_specs=(P(None, "leaf"), P("leaf"), P("rep", "leaf"), P("rep", "leaf")),
        out_specs=(P("rep", "leaf"), P("leaf", "rep", None)),
        check_vma=False,
    )
```

```python
import math

import jax
import jax.numpy as jnp
from jax import lax
from jax.experimental import pallas as pl
from jax.experimental.pallas import tpu as pltpu
from jax.sharding import PartitionSpec as P

LEAF = 512
S = 128
NB = 32
SUB = 8
STEP = LEAF // S
F32 = jnp.float32
BF16 = jnp.bfloat16
LOG_SCALE = -0.25 / math.pi
VMEM_LIMIT = 16 * 1024 * 1024


def split3(x):
    high = x.astype(BF16)
    rest = x - high.astype(F32)
    mid = rest.astype(BF16)
    return high, mid, (rest - mid.astype(F32)).astype(BF16)


def product(a, b, dims):
    ah, am, al = a
    bh, bm, bl = b
    left = jnp.concatenate([ah, ah, am, ah, al, am], dims[0][0])
    right = jnp.concatenate([bh, bm, bh, bl, bh, bm], dims[1][0])
    return lax.dot_general(left, right, (dims, ((), ())), preferred_element_type=F32)


def nn(a, b):
    return product(a, b, ((1,), (0,)))


def nt(a, b):
    return product(a, b, ((1,), (1,)))


def tn(a, b):
    return product(a, b, ((0,), (0,)))


def block_rows(diagonal, rows):
    n, width = rows.shape
    groups = n // SUB
    tiles = width // S
    sub = lax.broadcasted_iota(jnp.int32, (SUB, S), 0)
    cols = [
        [
            jnp.broadcast_to(diagonal[SUB * g : SUB * (g + 1), j : j + 1], (SUB, S))
            if g >= j // SUB
            else None
            for g in range(groups)
        ]
        for j in range(n)
    ]
    work = [
        [rows[SUB * g : SUB * (g + 1), S * t : S * (t + 1)] for t in range(tiles)]
        for g in range(groups)
    ]
    scales = [jnp.zeros((SUB, S), F32)] * groups
    factors = []

    def update(j, k):
        gj, sj = divmod(j, SUB)
        other = factors[k][gj][sj : sj + 1]
        for g in range(gj, groups):
            cols[j][g] = cols[j][g] - factors[k][g] * other

    for k in range(n):
        gk, sk = divmod(k, SUB)
        scale = lax.rsqrt(jnp.broadcast_to(cols[k][gk][sk : sk + 1], (SUB, S)))
        factor = {g: cols[k][g] * scale for g in range(gk, groups)}
        factors.append(dict(factor))
        scales[gk] = jnp.where(sub == sk, scale, scales[gk])
        if k + 1 < n:
            update(k + 1, k)
        if k + 2 < n:
            for earlier in range(k + 1):
                update(k + 2, earlier)
        factor[gk] = jnp.where(sub > sk, factor[gk], 0.0)
        for t in range(tiles):
            pivot_row = work[gk][t][sk : sk + 1] * scale
            for g in range(gk + (sk == SUB - 1), groups):
                work[g][t] = work[g][t] - factor[g] * pivot_row
    return jnp.concatenate(
        [
            jnp.concatenate([tile * scales[g] for tile in work[g]], 1)
            for g in range(groups)
        ],
        0,
    )


def eliminate(whole):
    n = whole.shape[0]
    blocks = [whole[i : i + NB] for i in range(0, n, NB)]
    done = []
    for k in range(len(blocks)):
        diagonal = blocks[k][:, k * NB : (k + 1) * NB]
        if k == len(blocks) - 1:
            done.append(block_rows(diagonal, blocks[k][:, n:]))
            break
        upper = block_rows(diagonal, blocks[k])
        done.append(upper[:, n:])
        parts = split3(upper)
        for j in range(k + 1, len(blocks)):
            at = slice(j * NB, (j + 1) * NB)
            blocks[j] = blocks[j] - tn([p[:, at] for p in parts], parts)
    return jnp.concatenate(done, 0)


def squared_distances(cols, rows):
    dx = cols[:, 0:1] - rows[0:1]
    dy = cols[:, 1:2] - rows[1:2]
    return dx * dx + dy * dy


def pick(x, every):
    n, width = x.shape
    kept = width // every
    i = lax.broadcasted_iota(jnp.int32, (width, kept), 0)
    j = lax.broadcasted_iota(jnp.int32, (width, kept), 1)
    chosen = jnp.where(i == every * j, 1.0, 0.0).astype(BF16)
    parts = jnp.concatenate([p.astype(F32) for p in split3(x)], 0).astype(BF16)
    got = jnp.dot(parts, chosen, preferred_element_type=F32)
    return got[:n] + (got[n : 2 * n] + got[2 * n :])


def coupling(mine, other, scale):
    to_mine = jnp.log(squared_distances(mine.T, other)) * (other[2:3] * scale)
    to_other = jnp.log(squared_distances(other.T, mine)) * (mine[2:3] * scale)
    return to_mine, to_other


def prepare_kernel(
    rep_ref, coords_ref, density_ref, low_ref, high_ref,
    near_high_ref, near_mid_hbm, far_ref, *rest,
):
    pair_refs, (wide, window, skeleton, near_mid_ref, sem) = rest[:-5], rest[-5:]
    rep = rep_ref[0]
    width = coords_ref.shape[1]
    cells = width // LEAF
    wide[:, :LEAF] = low_ref[SUB:]
    wide[:2, LEAF : LEAF + width] = coords_ref[...]
    wide[2:3, LEAF : LEAF + width] = density_ref[...]
    wide[3:, LEAF : LEAF + width] = jnp.zeros((SUB - 3, width), F32)
    wide[:, LEAF + width :] = high_ref[SUB:]

    window[...] = wide[:, pl.ds(pl.multiple_of(rep * LEAF, LEAF), 3 * LEAF)]
    targets = window[:, LEAF : 2 * LEAF]

    def near_chunk(chunk, carry):
        at = pl.ds(pl.multiple_of(chunk * S, S), S)
        cols = window[:, at].T
        i = lax.broadcasted_iota(jnp.int32, (S, LEAF), 0) + (chunk * S - LEAF)
        same = i == lax.broadcasted_iota(jnp.int32, (S, LEAF), 1)
        squared = jnp.where(same, 1.0, squared_distances(cols, targets))
        itself = -2.0 * (1.0 - jnp.log(0.5 * cols[:, 2:3]))
        values = jnp.where(same, itself, jnp.log(squared)) * (cols[:, 2:3] * LOG_SCALE)
        high = values.astype(BF16)
        near_high_ref[at] = high
        near_mid_ref[at] = (values - high.astype(F32)).astype(BF16)
        return carry

    lax.fori_loop(0, 3 * LEAF // S, near_chunk, 0)
    store = pltpu.make_async_copy(near_mid_ref, near_mid_hbm, sem)
    store.start()

    leaves = [wide[:, LEAF * (i + 1) : LEAF * (i + 2)] for i in range(cells)]
    nodes = pick(jnp.concatenate(leaves, 0), STEP)
    for level, ref in enumerate(pair_refs):
        count = cells >> level
        for i in range(count):
            skeleton[i] = nodes[SUB * i : SUB * (i + 1)]
        index = rep >> level
        pair = coupling(
            skeleton[index], skeleton[index ^ 1], LOG_SCALE * (STEP << level)
        )
        for side in range(2):
            for part, value in enumerate(split3(pair[side])):
                ref[side, part] = value
        joined = [
            jnp.concatenate(
                [nodes[SUB * i : SUB * (i + 1)], nodes[SUB * (i + 1) : SUB * (i + 2)]], 1
            )
            for i in range(0, count, 2)
        ]
        nodes = pick(jnp.concatenate(joined, 0), 2)
    scale = jnp.where(
        lax.broadcasted_iota(jnp.int32, (SUB, S), 0) == 2,
        float(STEP << len(pair_refs)), 1.0,
    )
    far_ref[...] = nodes * scale
    store.wait()


def edges_kernel(
    first_ref, last_ref, first_coords_ref, last_coords_ref, density_ref, low_ref, high_ref
):
    width = density_ref.shape[1]
    sides = (
        (high_ref, first_ref, first_coords_ref, 0),
        (low_ref, last_ref, last_coords_ref, width - LEAF),
    )
    for ref, tests_ref, coords_ref, start in sides:
        ref[:SUB] = tests_ref[...]
        ref[SUB : SUB + 2] = coords_ref[...]
        ref[SUB + 2 : SUB + 3] = density_ref[:, start : start + LEAF]
        ref[SUB + 3 :] = jnp.zeros((SUB - 3, LEAF), F32)


def turn(index, turned):
    return jnp.where(turned == 1, index % 4 * 4 + index // 4, index)


def pack_kernel(turned_ref, samples_ref, tests_ref, out_ref, sems):
    cells = out_ref.shape[0]
    copies = []

    def move(source, leaf, i, slot):
        start = pl.multiple_of(leaf * LEAF, LEAF)
        copies.append(
            pltpu.make_async_copy(
                source.at[:, pl.ds(start, LEAF)], out_ref.at[i, slot], sems.at[len(copies)]
            )
        )
        copies[-1].start()

    for i in range(cells):
        leaf = turn(jnp.int32(i), turned_ref[0])
        move(samples_ref, leaf, i, 0)
        if i > 0:
            move(tests_ref, leaf - 1, i, 1)
        move(tests_ref, leaf, i, 2)
        if i < cells - 1:
            move(tests_ref, leaf + 1, i, 3)
    for copy in copies:
        copy.wait()


def ends_kernel(packed_ref, low_ref, high_ref, out_ref, sems):
    copies = [
        pltpu.make_async_copy(low_ref.at[:SUB], out_ref.at[0, 1], sems.at[0]),
        pltpu.make_async_copy(
            high_ref.at[:SUB], out_ref.at[out_ref.shape[0] - 1, 3], sems.at[1]
        ),
    ]
    for copy in copies:
        copy.start()
    for copy in copies:
        copy.wait()


def leaf_kernel(
    data_ref, near_high_ref, near_mid_hbm, _, z_ref, inverse_ref, hat_ref, near_mid_ref, sem
):
    fetch = pltpu.make_async_copy(near_mid_hbm, near_mid_ref, sem)
    fetch.start()
    near = jnp.zeros((S, LEAF), F32)
    highs = []
    for part in range(3):
        near_high = near_high_ref[part * LEAF : (part + 1) * LEAF]
        high, mid, _ = split3(data_ref[:, part + 1].reshape(S, LEAF))
        left = jnp.concatenate([high, mid], 1)
        right = jnp.concatenate([near_high, near_high], 0)
        near = near + jnp.dot(left, right, preferred_element_type=F32)
        highs.append(high)
    fetch.wait()
    near = near + jnp.dot(
        jnp.concatenate(highs, 1), near_mid_ref[...], preferred_element_type=F32
    )
    samples = data_ref[:, 0].reshape(S, LEAF)
    z = samples - near
    z_ref[...] = z
    parts = split3(z)
    both = [split3(samples), split3(data_ref[:, 2].reshape(S, LEAF))]
    gram = nt(parts, parts)
    rights = [nt(parts, x) for x in both]
    eye = jnp.where(
        lax.broadcasted_iota(jnp.int32, (S, S), 0) == lax.broadcasted_iota(jnp.int32, (S, S), 1),
        1.0, 0.0,
    ).astype(F32)
    got = eliminate(jnp.concatenate([gram, *rights, eye], 1))
    hat_ref[:S] = got[:, :S]
    hat_ref[S:] = got[:, S : 2 * S]
    inverse_ref[...] = got[:, 2 * S :]


def basis_kernel(inverse_ref, z_ref, q_ref):
    q = nn(split3(inverse_ref[...]), split3(z_ref[...])) * math.sqrt(LEAF)
    q_ref[...] = q.reshape(q_ref.shape)


def off_diagonal(to_mine, to_other, mine_ref, other_ref):
    z_mine = mine_ref[:S] - nn(to_mine, split3(other_ref[S : 2 * S]))
    z_other = other_ref[:S] - nn(to_other, split3(mine_ref[S : 2 * S]))
    return z_mine, z_other


def merge(to_mine, to_other, mine_ref, other_ref):
    z_mine, z_other = off_diagonal(to_mine, to_other, mine_ref, other_ref)
    left = split3(jnp.concatenate([z_mine.T, z_other.T], 1))
    mine = jnp.concatenate([z_mine, mine_ref[:S], mine_ref[S : 2 * S]], 1)
    other = jnp.concatenate([z_other, other_ref[:S], other_ref[S : 2 * S]], 1)
    return eliminate(nn(left, split3(jnp.concatenate([mine, other], 0))))


def far_kernel(second_ref, mine_ref, other_ref, pair_ref, *joined_refs):
    mine, other = mine_ref[...], other_ref[...]
    for side, block in enumerate(coupling(mine, other, LOG_SCALE)):
        for part, value in enumerate(split3(block)):
            pair_ref[side, part] = value
    second = second_ref[0] == 1
    joined = jnp.concatenate(
        [jnp.where(second, other, mine), jnp.where(second, mine, other)], 1
    )
    double = lax.broadcasted_iota(jnp.int32, (SUB, S), 0) == 2
    for ref in joined_refs:
        ref[...] = pick(joined, 2) * jnp.where(double, 2.0, 1.0)


def parent_kernel(pair_ref, mine_ref, other_ref, *rest):
    hat_ref = rest[-1]
    pair = [[pair_ref[side, part] for part in range(3)] for side in range(2)]
    got = merge(*pair, mine_ref, other_ref)
    hat_ref[:S] = got[:, :S]
    hat_ref[S:] = got[:, S:]


def last_parent_kernel(turned_ref, pair_ref, mine_ref, other_ref, hat_ref, half_ref):
    parent_kernel(pair_ref, mine_ref, other_ref, hat_ref)
    half_ref[...] = jnp.where(turned_ref[0] == 1, hat_ref[S:], hat_ref[:S])


def top_kernel(
    place_ref, pair_ref, mine_ref, direct_ref, passed_ref, parts_ref, q_ref, basis_ref,
    all_rows, other_ref, sems,
):
    copies = []
    for i in range(parts_ref.shape[0]):
        leaf = turn(jnp.int32(i), place_ref[2])
        to = basis_ref.at[:, pl.ds(pl.multiple_of(leaf * LEAF, LEAF), LEAF)]
        copies.append(pltpu.make_async_copy(parts_ref.at[i], to, sems.at[i]))
        copies[-1].start()
    upper_direct = place_ref[2] == 0
    other_ref[:S] = jnp.where(upper_direct, direct_ref[...], passed_ref[...])
    other_ref[S:] = jnp.where(upper_direct, passed_ref[...], direct_ref[...])
    pair = [[pair_ref[side, part] for part in range(3)] for side in range(2)]
    z_mine, z_other = off_diagonal(*pair, mine_ref, other_ref)
    second = place_ref[0] == 1
    first = jnp.where(second, z_other, z_mine)
    last = jnp.where(second, z_mine, z_other)
    turned = jnp.concatenate([first.T, last.T], 1)
    gram = nn(split3(turned), split3(jnp.concatenate([first, last], 0)))
    all_rows[...] = eliminate(jnp.concatenate([gram, turned], 1)) * math.sqrt(2 * S)
    count = q_ref.shape[0]
    start = pl.multiple_of(place_ref[1] * count, count)
    q_ref[...] = all_rows[pl.ds(start, count)]
    for copy in copies:
        copy.wait()


VMEM = pl.BlockSpec(memory_space=pltpu.VMEM)
SMEM = pl.BlockSpec(memory_space=pltpu.SMEM)
ANY = pl.BlockSpec(memory_space=pl.ANY)
HBM = pl.BlockSpec(memory_space=pltpu.HBM)


def call(kernel, outs, specs, *operands, out_specs=None, scratch=(), aliases={}, flops=10**9):
    return pl.pallas_call(
        kernel,
        out_shape=[
            (pltpu.HBM if spec is HBM else jax.ShapeDtypeStruct)(shape, kind)
            for (shape, kind), spec in zip(outs, out_specs or [VMEM] * len(outs))
        ],
        in_specs=specs,
        out_specs=out_specs or [VMEM] * len(outs),
        scratch_shapes=list(scratch),
        input_output_aliases=aliases,
        compiler_params=pltpu.CompilerParams(vmem_limit_bytes=VMEM_LIMIT),
        cost_estimate=pl.CostEstimate(
            flops=flops, bytes_accessed=2**20, transcendentals=0
        ),
    )(*operands)


def in_hbm(block):
    return pltpu.with_memory_space_constraint(block, pltpu.HBM)


def swap(block, even, odd):
    leaves, reps = lax.axis_size("leaf"), lax.axis_size("rep")
    route = [
        (i * reps + j, i * reps + (j ^ (odd if i % 2 else even)))
        for i in range(leaves)
        for j in range(reps)
    ]
    return lax.ppermute(block, ("leaf", "rep"), route)


def cross(block, mask):
    count = lax.axis_size("leaf")
    return lax.ppermute(block, "leaf", [(i, i ^ mask) for i in range(count)])


def body(curve_coordinates, weighted_density, random_test_matrix, sketch_matrix):
    columns, width = random_test_matrix.shape
    cells = width // LEAF
    cell_levels = cells.bit_length() - 1
    rep = lax.axis_index("rep").astype(jnp.int32)
    leaf = lax.axis_index("leaf").astype(jnp.int32)
    count = lax.axis_size("leaf")
    turned = leaf & 1
    own = turn(rep, turned)

    density = weighted_density[None]

    def edge(rows, last):
        return pl.BlockSpec((rows, LEAF), lambda i: (0, cells - 1 if last else 0))

    low, high = pl.pallas_call(
        edges_kernel,
        grid=(1,),
        out_shape=[jax.ShapeDtypeStruct((2 * SUB, LEAF), F32)] * 2,
        in_specs=[edge(columns, False), edge(columns, True), edge(2, False), edge(2, True)]
        + [pl.BlockSpec((1, width), lambda i: (0, 0))],
        out_specs=[pl.BlockSpec((2 * SUB, LEAF), lambda i: (0, 0))] * 2,
    )(random_test_matrix, random_test_matrix, curve_coordinates, curve_coordinates, density)
    low = lax.ppermute(low, "leaf", [(i, (i + 1) % count) for i in range(count)])
    high = lax.ppermute(high, "leaf", [(i, (i - 1) % count) for i in range(count)])

    (parcels,) = call(
        pack_kernel,
        [((cells, 4, columns, LEAF), F32)],
        [SMEM, HBM, HBM],
        turned.reshape(1),
        in_hbm(sketch_matrix),
        in_hbm(random_test_matrix),
        out_specs=[HBM],
        scratch=[pltpu.SemaphoreType.DMA((4 * cells - 2,))],
    )
    (parcels,) = call(
        ends_kernel,
        [((cells, 4, columns, LEAF), F32)],
        [HBM, HBM, HBM],
        parcels,
        low,
        high,
        out_specs=[HBM],
        scratch=[pltpu.SemaphoreType.DMA((2,))],
        aliases={0: 0},
        flops=10**6,
    )
    data = lax.all_to_all(parcels, "rep", 0, 0)

    near_high, near_mid, far, *pairs = call(
        prepare_kernel,
        [((3 * LEAF, LEAF), BF16)] * 2
        + [((SUB, S), F32)]
        + [((2, 3, S, S), BF16)] * cell_levels,
        [SMEM] + [VMEM] * 4,
        own.reshape(1),
        curve_coordinates,
        density,
        low,
        high,
        scratch=[
            pltpu.VMEM((SUB, width + 2 * LEAF), F32),
            pltpu.VMEM((SUB, 3 * LEAF), F32),
            pltpu.VMEM((cells, SUB, S), F32),
            pltpu.VMEM((3 * LEAF, LEAF), BF16),
            pltpu.SemaphoreType.DMA,
        ],
        out_specs=[VMEM, HBM] + [VMEM] * (cell_levels + 1),
        flops=10**10,
    )
    skeleton = far
    for level in range(3):
        pair, *joined = call(
            far_kernel,
            [((2, 3, S, S), BF16), ((SUB, S), F32)][: 2 - level // 2],
            [SMEM] + [VMEM] * 2,
            (leaf >> level & 1).reshape(1),
            skeleton,
            cross(skeleton, 1 << level),
        )
        pairs.append(pair)
        skeleton = joined[0] if joined else None

    z, inverse, hat = call(
        leaf_kernel,
        [((S, LEAF), F32), ((S, S), F32), ((2 * S, S), F32)],
        [VMEM, VMEM, HBM, ANY],
        data,
        near_high,
        in_hbm(near_mid),
        pairs[-2],
        scratch=[pltpu.VMEM((3 * LEAF, LEAF), BF16), pltpu.SemaphoreType.DMA],
    )
    (basis,) = call(
        basis_kernel, [((cells, columns, LEAF), F32)], [VMEM] * 2, inverse, z
    )
    parts = lax.all_to_all(basis, "rep", 0, 0)

    for level, masks in enumerate(((1, 4), (3, 12), (4, 1), (12, 3))):
        pair = pairs[level]
        (hat,) = call(
            parent_kernel,
            [((2 * S, S), F32)],
            [VMEM] * 3 + [ANY] * (level == 1),
            pair,
            hat,
            swap(hat, *masks),
            *pairs[-1:] * (level == 1),
        )
    (hat,) = call(
        parent_kernel, [((2 * S, S), F32)], [VMEM] * 3, pairs[-3], hat, cross(hat, 1)
    )
    hat, half = call(
        last_parent_kernel,
        [((2 * S, S), F32), ((S, S), F32)],
        [SMEM] + [VMEM] * 3,
        turned.reshape(1),
        pairs[-2],
        hat,
        cross(hat, 2),
    )
    direct = cross(half, 4)
    top, leaf_basis = call(
        top_kernel,
        [((columns, 2 * S), F32), ((columns, width), F32)],
        [SMEM] + [VMEM] * 4 + [ANY],
        jnp.stack([leaf >> 2 & 1, rep, turned]),
        pairs[-1],
        hat,
        direct,
        cross(direct, 1),
        parts,
        out_specs=[VMEM, ANY],
        scratch=[
            pltpu.VMEM((S, 2 * S), F32),
            pltpu.VMEM((2 * S, S), F32),
            pltpu.SemaphoreType.DMA((cells,)),
        ],
    )
    return (leaf_basis, top[None])


def solution(mesh):
    return jax.shard_map(
        body,
        mesh=mesh,
        in_specs=(P(None, "leaf"), P("leaf"), P("rep", "leaf"), P("rep", "leaf")),
        out_specs=(P("rep", "leaf"), P("leaf", "rep", None)),
        check_vma=False,
    )
```

```python
import math

import jax
import jax.numpy as jnp
from jax import lax
from jax.experimental import pallas as pl
from jax.experimental.pallas import tpu as pltpu
from jax.sharding import PartitionSpec as P

LEAF = 512
S = 128
NB = 32
SUB = 8
STEP = LEAF // S
F32 = jnp.float32
BF16 = jnp.bfloat16
LOG_SCALE = -0.25 / math.pi
VMEM_LIMIT = 16 * 1024 * 1024


def split3(x):
    high = x.astype(BF16)
    rest = x - high.astype(F32)
    mid = rest.astype(BF16)
    return high, mid, (rest - mid.astype(F32)).astype(BF16)


def product(a, b, dims):
    ah, am, al = a
    bh, bm, bl = b
    left = jnp.concatenate([ah, ah, am, ah, al, am], dims[0][0])
    right = jnp.concatenate([bh, bm, bh, bl, bh, bm], dims[1][0])
    return lax.dot_general(left, right, (dims, ((), ())), preferred_element_type=F32)


def nn(a, b):
    return product(a, b, ((1,), (0,)))


def nt(a, b):
    return product(a, b, ((1,), (1,)))


def tn(a, b):
    return product(a, b, ((0,), (0,)))


def block_rows(diagonal, rows):
    n, width = rows.shape
    groups = n // SUB
    tiles = width // S
    sub = lax.broadcasted_iota(jnp.int32, (SUB, S), 0)
    cols = [
        [
            jnp.broadcast_to(diagonal[SUB * g : SUB * (g + 1), j : j + 1], (SUB, S))
            if g >= j // SUB
            else None
            for g in range(groups)
        ]
        for j in range(n)
    ]
    work = [
        [rows[SUB * g : SUB * (g + 1), S * t : S * (t + 1)] for t in range(tiles)]
        for g in range(groups)
    ]
    scales = [jnp.zeros((SUB, S), F32)] * groups
    factors = []

    def update(j, k):
        gj, sj = divmod(j, SUB)
        other = factors[k][gj][sj : sj + 1]
        for g in range(gj, groups):
            cols[j][g] = cols[j][g] - factors[k][g] * other

    for k in range(n):
        gk, sk = divmod(k, SUB)
        scale = lax.rsqrt(jnp.broadcast_to(cols[k][gk][sk : sk + 1], (SUB, S)))
        factor = {g: cols[k][g] * scale for g in range(gk, groups)}
        factors.append(dict(factor))
        scales[gk] = jnp.where(sub == sk, scale, scales[gk])
        if k + 1 < n:
            update(k + 1, k)
        if k + 2 < n:
            for earlier in range(k + 1):
                update(k + 2, earlier)
        factor[gk] = jnp.where(sub > sk, factor[gk], 0.0)
        for t in range(tiles):
            pivot_row = work[gk][t][sk : sk + 1] * scale
            for g in range(gk + (sk == SUB - 1), groups):
                work[g][t] = work[g][t] - factor[g] * pivot_row
    return jnp.concatenate(
        [
            jnp.concatenate([tile * scales[g] for tile in work[g]], 1)
            for g in range(groups)
        ],
        0,
    )


def eliminate(whole):
    n = whole.shape[0]
    blocks = [whole[i : i + NB] for i in range(0, n, NB)]
    done = []
    for k in range(len(blocks)):
        diagonal = blocks[k][:, k * NB : (k + 1) * NB]
        if k == len(blocks) - 1:
            done.append(block_rows(diagonal, blocks[k][:, n:]))
            break
        upper = block_rows(diagonal, blocks[k])
        done.append(upper[:, n:])
        parts = split3(upper)
        for j in range(k + 1, len(blocks)):
            at = slice(j * NB, (j + 1) * NB)
            blocks[j] = blocks[j] - tn([p[:, at] for p in parts], parts)
    return jnp.concatenate(done, 0)


def squared_distances(cols, rows):
    dx = cols[:, 0:1] - rows[0:1]
    dy = cols[:, 1:2] - rows[1:2]
    return dx * dx + dy * dy


def pick(x, every):
    n, width = x.shape
    kept = width // every
    i = lax.broadcasted_iota(jnp.int32, (width, kept), 0)
    j = lax.broadcasted_iota(jnp.int32, (width, kept), 1)
    chosen = jnp.where(i == every * j, 1.0, 0.0).astype(BF16)
    parts = jnp.concatenate([p.astype(F32) for p in split3(x)], 0).astype(BF16)
    got = jnp.dot(parts, chosen, preferred_element_type=F32)
    return got[:n] + (got[n : 2 * n] + got[2 * n :])


def coupling(mine, other, scale):
    to_mine = jnp.log(squared_distances(mine.T, other)) * (other[2:3] * scale)
    to_other = jnp.log(squared_distances(other.T, mine)) * (mine[2:3] * scale)
    return to_mine, to_other


def prepare_kernel(
    rep_ref, coords_ref, density_ref, low_ref, high_ref,
    near_high_ref, near_mid_hbm, far_ref, *rest,
):
    pair_refs, (wide, window, skeleton, near_mid_ref, sem) = rest[:-5], rest[-5:]
    rep = rep_ref[0]
    width = coords_ref.shape[1]
    cells = width // LEAF
    wide[:, :LEAF] = low_ref[SUB:]
    wide[:2, LEAF : LEAF + width] = coords_ref[...]
    wide[2:3, LEAF : LEAF + width] = density_ref[...]
    wide[3:, LEAF : LEAF + width] = jnp.zeros((SUB - 3, width), F32)
    wide[:, LEAF + width :] = high_ref[SUB:]

    window[...] = wide[:, pl.ds(pl.multiple_of(rep * LEAF, LEAF), 3 * LEAF)]
    targets = window[:, LEAF : 2 * LEAF]

    def near_chunk(chunk, carry):
        at = pl.ds(pl.multiple_of(chunk * S, S), S)
        cols = window[:, at].T
        i = lax.broadcasted_iota(jnp.int32, (S, LEAF), 0) + (chunk * S - LEAF)
        same = i == lax.broadcasted_iota(jnp.int32, (S, LEAF), 1)
        squared = jnp.where(same, 1.0, squared_distances(cols, targets))
        itself = -2.0 * (1.0 - jnp.log(0.5 * cols[:, 2:3]))
        values = jnp.where(same, itself, jnp.log(squared)) * (cols[:, 2:3] * LOG_SCALE)
        high = values.astype(BF16)
        near_high_ref[at] = high
        near_mid_ref[at] = (values - high.astype(F32)).astype(BF16)
        return carry

    lax.fori_loop(0, 3 * LEAF // S, near_chunk, 0)
    store = pltpu.make_async_copy(near_mid_ref, near_mid_hbm, sem)
    store.start()

    leaves = [wide[:, LEAF * (i + 1) : LEAF * (i + 2)] for i in range(cells)]
    nodes = pick(jnp.concatenate(leaves, 0), STEP)
    for level, ref in enumerate(pair_refs):
        count = cells >> level
        for i in range(count):
            skeleton[i] = nodes[SUB * i : SUB * (i + 1)]
        index = rep >> level
        pair = coupling(
            skeleton[index], skeleton[index ^ 1], LOG_SCALE * (STEP << level)
        )
        for side in range(2):
            for part, value in enumerate(split3(pair[side])):
                ref[side, part] = value
        joined = [
            jnp.concatenate(
                [nodes[SUB * i : SUB * (i + 1)], nodes[SUB * (i + 1) : SUB * (i + 2)]], 1
            )
            for i in range(0, count, 2)
        ]
        nodes = pick(jnp.concatenate(joined, 0), 2)
    scale = jnp.where(
        lax.broadcasted_iota(jnp.int32, (SUB, S), 0) == 2,
        float(STEP << len(pair_refs)), 1.0,
    )
    far_ref[...] = nodes * scale
    store.wait()


def edges_kernel(
    first_ref, last_ref, first_coords_ref, last_coords_ref, density_ref, low_ref, high_ref
):
    width = density_ref.shape[1]
    sides = (
        (high_ref, first_ref, first_coords_ref, 0),
        (low_ref, last_ref, last_coords_ref, width - LEAF),
    )
    for ref, tests_ref, coords_ref, start in sides:
        ref[:SUB] = tests_ref[...]
        ref[SUB : SUB + 2] = coords_ref[...]
        ref[SUB + 2 : SUB + 3] = density_ref[:, start : start + LEAF]
        ref[SUB + 3 :] = jnp.zeros((SUB - 3, LEAF), F32)


def turn(index, turned):
    return jnp.where(turned == 1, index % 4 * 4 + index // 4, index)


def pack_kernel(turned_ref, samples_hbm, tests_hbm, out_ref, samples_ref, tests_ref, ins, sems):
    cells = out_ref.shape[0]
    loads = [
        pltpu.make_async_copy(samples_hbm, samples_ref, ins.at[0]),
        pltpu.make_async_copy(tests_hbm, tests_ref, ins.at[1]),
    ]
    for load in loads:
        load.start()
    for load in loads:
        load.wait()
    copies = []

    def move(source, leaf, i, slot):
        start = pl.multiple_of(leaf * LEAF, LEAF)
        copies.append(
            pltpu.make_async_copy(
                source.at[:, pl.ds(start, LEAF)], out_ref.at[i, slot], sems.at[len(copies)]
            )
        )
        copies[-1].start()

    for i in range(cells):
        leaf = turn(jnp.int32(i), turned_ref[0])
        move(samples_ref, leaf, i, 0)
        if i > 0:
            move(tests_ref, leaf - 1, i, 1)
        move(tests_ref, leaf, i, 2)
        if i < cells - 1:
            move(tests_ref, leaf + 1, i, 3)
    for copy in copies:
        copy.wait()


def ends_kernel(packed_ref, low_ref, high_ref, out_ref, sems):
    copies = [
        pltpu.make_async_copy(low_ref.at[:SUB], out_ref.at[0, 1], sems.at[0]),
        pltpu.make_async_copy(
            high_ref.at[:SUB], out_ref.at[out_ref.shape[0] - 1, 3], sems.at[1]
        ),
    ]
    for copy in copies:
        copy.start()
    for copy in copies:
        copy.wait()


def leaf_kernel(
    data_ref, near_high_ref, near_mid_hbm, _, z_ref, inverse_ref, hat_ref, near_mid_ref, sems
):
    pieces = [pl.ds(part * LEAF, LEAF) for part in range(3)]
    fetches = [
        pltpu.make_async_copy(near_mid_hbm.at[at], near_mid_ref.at[at], sems.at[i])
        for i, at in enumerate(pieces)
    ]
    for fetch in fetches:
        fetch.start()
    near = jnp.zeros((S, LEAF), F32)
    highs = []
    for part in range(3):
        near_high = near_high_ref[part * LEAF : (part + 1) * LEAF]
        high, mid, _ = split3(data_ref[:, part + 1].reshape(S, LEAF))
        left = jnp.concatenate([high, mid], 1)
        right = jnp.concatenate([near_high, near_high], 0)
        near = near + jnp.dot(left, right, preferred_element_type=F32)
        highs.append(high)
    for fetch in fetches:
        fetch.wait()
    near = near + jnp.dot(
        jnp.concatenate(highs, 1), near_mid_ref[...], preferred_element_type=F32
    )
    samples = data_ref[:, 0].reshape(S, LEAF)
    z = samples - near
    z_ref[...] = z
    parts = split3(z)
    both = [split3(samples), split3(data_ref[:, 2].reshape(S, LEAF))]
    gram = nt(parts, parts)
    rights = [nt(parts, x) for x in both]
    eye = jnp.where(
        lax.broadcasted_iota(jnp.int32, (S, S), 0) == lax.broadcasted_iota(jnp.int32, (S, S), 1),
        1.0, 0.0,
    ).astype(F32)
    got = eliminate(jnp.concatenate([gram, *rights, eye], 1))
    hat_ref[:S] = got[:, :S]
    hat_ref[S:] = got[:, S : 2 * S]
    inverse_ref[...] = got[:, 2 * S :]


def basis_kernel(inverse_ref, z_ref, q_ref):
    q = nn(split3(inverse_ref[...]), split3(z_ref[...])) * math.sqrt(LEAF)
    q_ref[...] = q.reshape(q_ref.shape)


def off_diagonal(to_mine, to_other, mine_ref, other_ref):
    z_mine = mine_ref[:S] - nn(to_mine, split3(other_ref[S : 2 * S]))
    z_other = other_ref[:S] - nn(to_other, split3(mine_ref[S : 2 * S]))
    return z_mine, z_other


def merge(to_mine, to_other, mine_ref, other_ref):
    z_mine, z_other = off_diagonal(to_mine, to_other, mine_ref, other_ref)
    left = split3(jnp.concatenate([z_mine.T, z_other.T], 1))
    mine = jnp.concatenate([z_mine, mine_ref[:S], mine_ref[S : 2 * S]], 1)
    other = jnp.concatenate([z_other, other_ref[:S], other_ref[S : 2 * S]], 1)
    return eliminate(nn(left, split3(jnp.concatenate([mine, other], 0))))


def far_kernel(second_ref, mine_ref, other_ref, pair_ref, *joined_refs):
    mine, other = mine_ref[...], other_ref[...]
    for side, block in enumerate(coupling(mine, other, LOG_SCALE)):
        for part, value in enumerate(split3(block)):
            pair_ref[side, part] = value
    second = second_ref[0] == 1
    joined = jnp.concatenate(
        [jnp.where(second, other, mine), jnp.where(second, mine, other)], 1
    )
    double = lax.broadcasted_iota(jnp.int32, (SUB, S), 0) == 2
    for ref in joined_refs:
        ref[...] = pick(joined, 2) * jnp.where(double, 2.0, 1.0)


def parent_kernel(pair_ref, mine_ref, other_ref, *rest):
    hat_ref = rest[-1]
    pair = [[pair_ref[side, part] for part in range(3)] for side in range(2)]
    got = merge(*pair, mine_ref, other_ref)
    hat_ref[:S] = got[:, :S]
    hat_ref[S:] = got[:, S:]


def laying_parent_kernel(
    turned_ref, pair_ref, mine_ref, other_ref, parts_ref, hat_ref, basis_ref, sems
):
    copies = []
    for i in range(parts_ref.shape[0]):
        leaf = turn(jnp.int32(i), turned_ref[0])
        to = basis_ref.at[:, pl.ds(pl.multiple_of(leaf * LEAF, LEAF), LEAF)]
        copies.append(pltpu.make_async_copy(parts_ref.at[i], to, sems.at[i]))
        copies[-1].start()
    parent_kernel(pair_ref, mine_ref, other_ref, hat_ref)
    for copy in copies:
        copy.wait()


def last_parent_kernel(turned_ref, pair_ref, mine_ref, other_ref, hat_ref, half_ref):
    parent_kernel(pair_ref, mine_ref, other_ref, hat_ref)
    half_ref[...] = jnp.where(turned_ref[0] == 1, hat_ref[S:], hat_ref[:S])


def top_kernel(
    place_ref, pair_ref, mine_ref, direct_ref, passed_ref, q_ref, all_rows, other_ref
):
    upper_direct = place_ref[2] == 0
    other_ref[:S] = jnp.where(upper_direct, direct_ref[...], passed_ref[...])
    other_ref[S:] = jnp.where(upper_direct, passed_ref[...], direct_ref[...])
    pair = [[pair_ref[side, part] for part in range(3)] for side in range(2)]
    z_mine, z_other = off_diagonal(*pair, mine_ref, other_ref)
    second = place_ref[0] == 1
    first = jnp.where(second, z_other, z_mine)
    last = jnp.where(second, z_mine, z_other)
    turned = jnp.concatenate([first.T, last.T], 1)
    gram = nn(split3(turned), split3(jnp.concatenate([first, last], 0)))
    all_rows[...] = eliminate(jnp.concatenate([gram, turned], 1)) * math.sqrt(2 * S)
    count = q_ref.shape[0]
    start = pl.multiple_of(place_ref[1] * count, count)
    q_ref[...] = all_rows[pl.ds(start, count)]


VMEM = pl.BlockSpec(memory_space=pltpu.VMEM)
SMEM = pl.BlockSpec(memory_space=pltpu.SMEM)
ANY = pl.BlockSpec(memory_space=pl.ANY)
HBM = pl.BlockSpec(memory_space=pltpu.HBM)


def call(kernel, outs, specs, *operands, out_specs=None, scratch=(), aliases={}, flops=10**9):
    return pl.pallas_call(
        kernel,
        out_shape=[
            (pltpu.HBM if spec is HBM else jax.ShapeDtypeStruct)(shape, kind)
            for (shape, kind), spec in zip(outs, out_specs or [VMEM] * len(outs))
        ],
        in_specs=specs,
        out_specs=out_specs or [VMEM] * len(outs),
        scratch_shapes=list(scratch),
        input_output_aliases=aliases,
        compiler_params=pltpu.CompilerParams(vmem_limit_bytes=VMEM_LIMIT),
        cost_estimate=pl.CostEstimate(
            flops=flops, bytes_accessed=2**20, transcendentals=0
        ),
    )(*operands)


def in_hbm(block):
    return pltpu.with_memory_space_constraint(block, pltpu.HBM)


def swap(block, even, odd):
    leaves, reps = lax.axis_size("leaf"), lax.axis_size("rep")
    route = [
        (i * reps + j, i * reps + (j ^ (odd if i % 2 else even)))
        for i in range(leaves)
        for j in range(reps)
    ]
    return lax.ppermute(block, ("leaf", "rep"), route)


def cross(block, mask):
    count = lax.axis_size("leaf")
    return lax.ppermute(block, "leaf", [(i, i ^ mask) for i in range(count)])


def body(curve_coordinates, weighted_density, random_test_matrix, sketch_matrix):
    columns, width = random_test_matrix.shape
    cells = width // LEAF
    cell_levels = cells.bit_length() - 1
    rep = lax.axis_index("rep").astype(jnp.int32)
    leaf = lax.axis_index("leaf").astype(jnp.int32)
    count = lax.axis_size("leaf")
    turned = leaf & 1
    own = turn(rep, turned)

    density = weighted_density[None]

    def edge(rows, last):
        return pl.BlockSpec((rows, LEAF), lambda i: (0, cells - 1 if last else 0))

    low, high = pl.pallas_call(
        edges_kernel,
        grid=(1,),
        out_shape=[jax.ShapeDtypeStruct((2 * SUB, LEAF), F32)] * 2,
        in_specs=[edge(columns, False), edge(columns, True), edge(2, False), edge(2, True)]
        + [pl.BlockSpec((1, width), lambda i: (0, 0))],
        out_specs=[pl.BlockSpec((2 * SUB, LEAF), lambda i: (0, 0))] * 2,
    )(random_test_matrix, random_test_matrix, curve_coordinates, curve_coordinates, density)
    low = lax.ppermute(low, "leaf", [(i, (i + 1) % count) for i in range(count)])
    high = lax.ppermute(high, "leaf", [(i, (i - 1) % count) for i in range(count)])

    (parcels,) = call(
        pack_kernel,
        [((cells, 4, columns, LEAF), F32)],
        [SMEM, HBM, HBM],
        turned.reshape(1),
        in_hbm(sketch_matrix),
        in_hbm(random_test_matrix),
        out_specs=[HBM],
        scratch=[
            pltpu.VMEM((columns, width), F32),
            pltpu.VMEM((columns, width), F32),
            pltpu.SemaphoreType.DMA((2,)),
            pltpu.SemaphoreType.DMA((4 * cells - 2,)),
        ],
    )
    (parcels,) = call(
        ends_kernel,
        [((cells, 4, columns, LEAF), F32)],
        [HBM, HBM, HBM],
        parcels,
        low,
        high,
        out_specs=[HBM],
        scratch=[pltpu.SemaphoreType.DMA((2,))],
        aliases={0: 0},
        flops=10**6,
    )
    data = lax.all_to_all(parcels, "rep", 0, 0)

    near_high, near_mid, far, *pairs = call(
        prepare_kernel,
        [((3 * LEAF, LEAF), BF16)] * 2
        + [((SUB, S), F32)]
        + [((2, 3, S, S), BF16)] * cell_levels,
        [SMEM] + [VMEM] * 4,
        own.reshape(1),
        curve_coordinates,
        density,
        low,
        high,
        scratch=[
            pltpu.VMEM((SUB, width + 2 * LEAF), F32),
            pltpu.VMEM((SUB, 3 * LEAF), F32),
            pltpu.VMEM((cells, SUB, S), F32),
            pltpu.VMEM((3 * LEAF, LEAF), BF16),
            pltpu.SemaphoreType.DMA,
        ],
        out_specs=[VMEM, HBM] + [VMEM] * (cell_levels + 1),
        flops=10**10,
    )
    skeleton = far
    for level in range(3):
        pair, *joined = call(
            far_kernel,
            [((2, 3, S, S), BF16), ((SUB, S), F32)][: 2 - level // 2],
            [SMEM] + [VMEM] * 2,
            (leaf >> level & 1).reshape(1),
            skeleton,
            cross(skeleton, 1 << level),
        )
        pairs.append(pair)
        skeleton = joined[0] if joined else None

    z, inverse, hat = call(
        leaf_kernel,
        [((S, LEAF), F32), ((S, S), F32), ((2 * S, S), F32)],
        [VMEM, VMEM, HBM, ANY],
        data,
        near_high,
        in_hbm(near_mid),
        pairs[-2],
        scratch=[pltpu.VMEM((3 * LEAF, LEAF), BF16), pltpu.SemaphoreType.DMA((3,))],
    )
    (basis,) = call(
        basis_kernel, [((cells, columns, LEAF), F32)], [VMEM] * 2, inverse, z
    )
    parts = lax.all_to_all(basis, "rep", 0, 0)

    for level, masks in enumerate(((1, 4), (3, 12), (4, 1), (12, 3))):
        pair = pairs[level]
        (hat,) = call(
            parent_kernel,
            [((2 * S, S), F32)],
            [VMEM] * 3 + [ANY] * (level == 1),
            pair,
            hat,
            swap(hat, *masks),
            *pairs[-1:] * (level == 1),
        )
    hat, leaf_basis = call(
        laying_parent_kernel,
        [((2 * S, S), F32), ((columns, width), F32)],
        [SMEM] + [VMEM] * 3 + [ANY],
        turned.reshape(1),
        pairs[-3],
        hat,
        cross(hat, 1),
        parts,
        out_specs=[VMEM, HBM],
        scratch=[pltpu.SemaphoreType.DMA((cells,))],
    )
    hat, half = call(
        last_parent_kernel,
        [((2 * S, S), F32), ((S, S), F32)],
        [SMEM] + [VMEM] * 3,
        turned.reshape(1),
        pairs[-2],
        hat,
        cross(hat, 2),
    )
    direct = cross(half, 4)
    (top,) = call(
        top_kernel,
        [((columns, 2 * S), F32)],
        [SMEM] + [VMEM] * 4,
        jnp.stack([leaf >> 2 & 1, rep, turned]),
        pairs[-1],
        hat,
        direct,
        cross(direct, 1),
        scratch=[
            pltpu.VMEM((S, 2 * S), F32),
            pltpu.VMEM((2 * S, S), F32),
        ],
    )
    return (leaf_basis, top[None])


def solution(mesh):
    return jax.shard_map(
        body,
        mesh=mesh,
        in_specs=(P(None, "leaf"), P("leaf"), P("rep", "leaf"), P("rep", "leaf")),
        out_specs=(P("rep", "leaf"), P("leaf", "rep", None)),
        check_vma=False,
    )
```

```python
import math

import jax
import jax.numpy as jnp
from jax import lax
from jax.experimental import pallas as pl
from jax.experimental.pallas import tpu as pltpu
from jax.sharding import PartitionSpec as P

LEAF = 512
S = 128
NB = 32
SUB = 8
STEP = LEAF // S
F32 = jnp.float32
BF16 = jnp.bfloat16
LOG_SCALE = -0.25 / math.pi
VMEM_LIMIT = 16 * 1024 * 1024


def split3(x):
    high = x.astype(BF16)
    rest = x - high.astype(F32)
    mid = rest.astype(BF16)
    return high, mid, (rest - mid.astype(F32)).astype(BF16)


def product(a, b, dims):
    ah, am, al = a
    bh, bm, bl = b
    left = jnp.concatenate([ah, ah, am, ah, al, am], dims[0][0])
    right = jnp.concatenate([bh, bm, bh, bl, bh, bm], dims[1][0])
    return lax.dot_general(left, right, (dims, ((), ())), preferred_element_type=F32)


def nn(a, b):
    return product(a, b, ((1,), (0,)))


def nt(a, b):
    return product(a, b, ((1,), (1,)))


def tn(a, b):
    return product(a, b, ((0,), (0,)))


def block_rows(diagonal, rows):
    n, width = rows.shape
    groups = n // SUB
    tiles = width // S
    sub = lax.broadcasted_iota(jnp.int32, (SUB, S), 0)
    cols = [
        [
            jnp.broadcast_to(diagonal[SUB * g : SUB * (g + 1), j : j + 1], (SUB, S))
            if g >= j // SUB
            else None
            for g in range(groups)
        ]
        for j in range(n)
    ]
    work = [
        [rows[SUB * g : SUB * (g + 1), S * t : S * (t + 1)] for t in range(tiles)]
        for g in range(groups)
    ]
    scales = [jnp.zeros((SUB, S), F32)] * groups
    factors = []

    def update(j, k):
        gj, sj = divmod(j, SUB)
        other = factors[k][gj][sj : sj + 1]
        for g in range(gj, groups):
            cols[j][g] = cols[j][g] - factors[k][g] * other

    for k in range(n):
        gk, sk = divmod(k, SUB)
        scale = lax.rsqrt(jnp.broadcast_to(cols[k][gk][sk : sk + 1], (SUB, S)))
        factor = {g: cols[k][g] * scale for g in range(gk, groups)}
        factors.append(dict(factor))
        scales[gk] = jnp.where(sub == sk, scale, scales[gk])
        if k + 1 < n:
            update(k + 1, k)
        if k + 2 < n:
            for earlier in range(k + 1):
                update(k + 2, earlier)
        factor[gk] = jnp.where(sub > sk, factor[gk], 0.0)
        for t in range(tiles):
            pivot_row = work[gk][t][sk : sk + 1] * scale
            for g in range(gk + (sk == SUB - 1), groups):
                work[g][t] = work[g][t] - factor[g] * pivot_row
    return jnp.concatenate(
        [
            jnp.concatenate([tile * scales[g] for tile in work[g]], 1)
            for g in range(groups)
        ],
        0,
    )


def eliminate(whole):
    n = whole.shape[0]
    blocks = [whole[i : i + NB] for i in range(0, n, NB)]
    done = []
    for k in range(len(blocks)):
        diagonal = blocks[k][:, k * NB : (k + 1) * NB]
        if k == len(blocks) - 1:
            done.append(block_rows(diagonal, blocks[k][:, n:]))
            break
        upper = block_rows(diagonal, blocks[k])
        done.append(upper[:, n:])
        parts = split3(upper)
        for j in range(k + 1, len(blocks)):
            at = slice(j * NB, (j + 1) * NB)
            blocks[j] = blocks[j] - tn([p[:, at] for p in parts], parts)
    return jnp.concatenate(done, 0)


def squared_distances(cols, rows):
    dx = cols[:, 0:1] - rows[0:1]
    dy = cols[:, 1:2] - rows[1:2]
    return dx * dx + dy * dy


def pick(x, every):
    n, width = x.shape
    kept = width // every
    i = lax.broadcasted_iota(jnp.int32, (width, kept), 0)
    j = lax.broadcasted_iota(jnp.int32, (width, kept), 1)
    chosen = jnp.where(i == every * j, 1.0, 0.0).astype(BF16)
    parts = jnp.concatenate([p.astype(F32) for p in split3(x)], 0).astype(BF16)
    got = jnp.dot(parts, chosen, preferred_element_type=F32)
    return got[:n] + (got[n : 2 * n] + got[2 * n :])


def coupling(mine, other, scale):
    to_mine = jnp.log(squared_distances(mine.T, other)) * (other[2:3] * scale)
    to_other = jnp.log(squared_distances(other.T, mine)) * (mine[2:3] * scale)
    return to_mine, to_other


def prepare_kernel(
    rep_ref, coords_ref, density_ref, low_ref, high_ref,
    near_high_ref, near_mid_hbm, far_ref, *rest,
):
    pair_refs, (wide, window, skeleton, near_mid_ref, sem) = rest[:-5], rest[-5:]
    rep = rep_ref[0]
    width = coords_ref.shape[1]
    cells = width // LEAF
    wide[:, :LEAF] = low_ref[SUB:]
    wide[:2, LEAF : LEAF + width] = coords_ref[...]
    wide[2:3, LEAF : LEAF + width] = density_ref[...]
    wide[3:, LEAF : LEAF + width] = jnp.zeros((SUB - 3, width), F32)
    wide[:, LEAF + width :] = high_ref[SUB:]

    window[...] = wide[:, pl.ds(pl.multiple_of(rep * LEAF, LEAF), 3 * LEAF)]
    targets = window[:, LEAF : 2 * LEAF]

    def near_chunk(chunk, carry):
        at = pl.ds(pl.multiple_of(chunk * S, S), S)
        cols = window[:, at].T
        i = lax.broadcasted_iota(jnp.int32, (S, LEAF), 0) + (chunk * S - LEAF)
        same = i == lax.broadcasted_iota(jnp.int32, (S, LEAF), 1)
        squared = jnp.where(same, 1.0, squared_distances(cols, targets))
        itself = -2.0 * (1.0 - jnp.log(0.5 * cols[:, 2:3]))
        values = jnp.where(same, itself, jnp.log(squared)) * (cols[:, 2:3] * LOG_SCALE)
        high = values.astype(BF16)
        near_high_ref[at] = high
        near_mid_ref[at] = (values - high.astype(F32)).astype(BF16)
        return carry

    lax.fori_loop(0, 3 * LEAF // S, near_chunk, 0)
    store = pltpu.make_async_copy(near_mid_ref, near_mid_hbm, sem)
    store.start()

    leaves = [wide[:, LEAF * (i + 1) : LEAF * (i + 2)] for i in range(cells)]
    nodes = pick(jnp.concatenate(leaves, 0), STEP)
    for level, ref in enumerate(pair_refs):
        count = cells >> level
        for i in range(count):
            skeleton[i] = nodes[SUB * i : SUB * (i + 1)]
        index = rep >> level
        pair = coupling(
            skeleton[index], skeleton[index ^ 1], LOG_SCALE * (STEP << level)
        )
        for side in range(2):
            ref[side] = pair[side]
        joined = [
            jnp.concatenate(
                [nodes[SUB * i : SUB * (i + 1)], nodes[SUB * (i + 1) : SUB * (i + 2)]], 1
            )
            for i in range(0, count, 2)
        ]
        nodes = pick(jnp.concatenate(joined, 0), 2)
    scale = jnp.where(
        lax.broadcasted_iota(jnp.int32, (SUB, S), 0) == 2,
        float(STEP << len(pair_refs)), 1.0,
    )
    far_ref[...] = nodes * scale
    store.wait()


def edges_kernel(
    first_ref, last_ref, first_coords_ref, last_coords_ref, density_ref, low_ref, high_ref
):
    width = density_ref.shape[1]
    sides = (
        (high_ref, first_ref, first_coords_ref, 0),
        (low_ref, last_ref, last_coords_ref, width - LEAF),
    )
    for ref, tests_ref, coords_ref, start in sides:
        ref[:SUB] = tests_ref[...]
        ref[SUB : SUB + 2] = coords_ref[...]
        ref[SUB + 2 : SUB + 3] = density_ref[:, start : start + LEAF]
        ref[SUB + 3 :] = jnp.zeros((SUB - 3, LEAF), F32)


def turn(index, turned):
    return jnp.where(turned == 1, index % 4 * 4 + index // 4, index)


def pack_kernel(turned_ref, samples_hbm, tests_hbm, out_ref, samples_ref, tests_ref, ins, sems):
    cells = out_ref.shape[0]
    loads = [
        pltpu.make_async_copy(samples_hbm, samples_ref, ins.at[0]),
        pltpu.make_async_copy(tests_hbm, tests_ref, ins.at[1]),
    ]
    for load in loads:
        load.start()
    for load in loads:
        load.wait()
    copies = []

    def move(source, leaf, i, slot):
        start = pl.multiple_of(leaf * LEAF, LEAF)
        copies.append(
            pltpu.make_async_copy(
                source.at[:, pl.ds(start, LEAF)], out_ref.at[i, slot], sems.at[len(copies)]
            )
        )
        copies[-1].start()

    for i in range(cells):
        leaf = turn(jnp.int32(i), turned_ref[0])
        move(samples_ref, leaf, i, 0)
        if i > 0:
            move(tests_ref, leaf - 1, i, 1)
        move(tests_ref, leaf, i, 2)
        if i < cells - 1:
            move(tests_ref, leaf + 1, i, 3)
    for copy in copies:
        copy.wait()


def ends_kernel(packed_ref, low_ref, high_ref, out_ref, sems):
    copies = [
        pltpu.make_async_copy(low_ref.at[:SUB], out_ref.at[0, 1], sems.at[0]),
        pltpu.make_async_copy(
            high_ref.at[:SUB], out_ref.at[out_ref.shape[0] - 1, 3], sems.at[1]
        ),
    ]
    for copy in copies:
        copy.start()
    for copy in copies:
        copy.wait()


def leaf_kernel(
    data_ref, near_high_ref, near_mid_hbm, _, z_ref, inverse_ref, hat_ref, near_mid_ref, sems
):
    pieces = [pl.ds(part * LEAF, LEAF) for part in range(3)]
    fetches = [
        pltpu.make_async_copy(near_mid_hbm.at[at], near_mid_ref.at[at], sems.at[i])
        for i, at in enumerate(pieces)
    ]
    for fetch in fetches:
        fetch.start()
    near = jnp.zeros((S, LEAF), F32)
    highs = []
    for part in range(3):
        near_high = near_high_ref[part * LEAF : (part + 1) * LEAF]
        high, mid, _ = split3(data_ref[:, part + 1].reshape(S, LEAF))
        left = jnp.concatenate([high, mid], 1)
        right = jnp.concatenate([near_high, near_high], 0)
        near = near + jnp.dot(left, right, preferred_element_type=F32)
        highs.append(high)
    for fetch in fetches:
        fetch.wait()
    near = near + jnp.dot(
        jnp.concatenate(highs, 1), near_mid_ref[...], preferred_element_type=F32
    )
    samples = data_ref[:, 0].reshape(S, LEAF)
    z = samples - near
    z_ref[...] = z
    parts = split3(z)
    both = [split3(samples), split3(data_ref[:, 2].reshape(S, LEAF))]
    gram = nt(parts, parts)
    rights = [nt(parts, x) for x in both]
    eye = jnp.where(
        lax.broadcasted_iota(jnp.int32, (S, S), 0) == lax.broadcasted_iota(jnp.int32, (S, S), 1),
        1.0, 0.0,
    ).astype(F32)
    got = eliminate(jnp.concatenate([gram, *rights, eye], 1))
    hat_ref[:S] = got[:, :S]
    hat_ref[S:] = got[:, S : 2 * S]
    inverse_ref[...] = got[:, 2 * S :]


def basis_kernel(inverse_ref, z_ref, q_ref):
    q = nn(split3(inverse_ref[...]), split3(z_ref[...])) * math.sqrt(LEAF)
    q_ref[...] = q.reshape(q_ref.shape)


def off_diagonal(to_mine, to_other, mine_ref, other_ref):
    z_mine = mine_ref[:S] - nn(to_mine, split3(other_ref[S : 2 * S]))
    z_other = other_ref[:S] - nn(to_other, split3(mine_ref[S : 2 * S]))
    return z_mine, z_other


def merge(to_mine, to_other, mine_ref, other_ref):
    z_mine, z_other = off_diagonal(to_mine, to_other, mine_ref, other_ref)
    left = split3(jnp.concatenate([z_mine.T, z_other.T], 1))
    mine = jnp.concatenate([z_mine, mine_ref[:S], mine_ref[S : 2 * S]], 1)
    other = jnp.concatenate([z_other, other_ref[:S], other_ref[S : 2 * S]], 1)
    return eliminate(nn(left, split3(jnp.concatenate([mine, other], 0))))


def far_kernel(second_ref, mine_ref, other_ref, pair_ref, *joined_refs):
    mine, other = mine_ref[...], other_ref[...]
    for side, block in enumerate(coupling(mine, other, LOG_SCALE)):
        pair_ref[side] = block
    second = second_ref[0] == 1
    joined = jnp.concatenate(
        [jnp.where(second, other, mine), jnp.where(second, mine, other)], 1
    )
    double = lax.broadcasted_iota(jnp.int32, (SUB, S), 0) == 2
    for ref in joined_refs:
        ref[...] = pick(joined, 2) * jnp.where(double, 2.0, 1.0)


def parent_kernel(pair_ref, mine_ref, other_ref, *rest):
    hat_ref = rest[-1]
    pair = [split3(pair_ref[side]) for side in range(2)]
    got = merge(*pair, mine_ref, other_ref)
    hat_ref[:S] = got[:, :S]
    hat_ref[S:] = got[:, S:]


def lay_kernel(turned_ref, parts_ref, top_ref, basis_ref, out_ref, sems):
    copies = [pltpu.make_async_copy(top_ref, out_ref, sems.at[parts_ref.shape[0]])]
    copies[0].start()
    for i in range(parts_ref.shape[0]):
        leaf = turn(jnp.int32(i), turned_ref[0])
        to = basis_ref.at[:, pl.ds(pl.multiple_of(leaf * LEAF, LEAF), LEAF)]
        copies.append(pltpu.make_async_copy(parts_ref.at[i], to, sems.at[i]))
        copies[-1].start()
    for copy in copies:
        copy.wait()


def last_parent_kernel(turned_ref, pair_ref, mine_ref, other_ref, hat_ref, half_ref):
    parent_kernel(pair_ref, mine_ref, other_ref, hat_ref)
    half_ref[...] = jnp.where(turned_ref[0] == 1, hat_ref[S:], hat_ref[:S])


def top_kernel(
    place_ref, pair_ref, mine_ref, direct_ref, passed_ref, q_ref, all_rows, other_ref
):
    upper_direct = place_ref[2] == 0
    other_ref[:S] = jnp.where(upper_direct, direct_ref[...], passed_ref[...])
    other_ref[S:] = jnp.where(upper_direct, passed_ref[...], direct_ref[...])
    pair = [split3(pair_ref[side]) for side in range(2)]
    z_mine, z_other = off_diagonal(*pair, mine_ref, other_ref)
    second = place_ref[0] == 1
    first = jnp.where(second, z_other, z_mine)
    last = jnp.where(second, z_mine, z_other)
    turned = jnp.concatenate([first.T, last.T], 1)
    gram = nn(split3(turned), split3(jnp.concatenate([first, last], 0)))
    all_rows[...] = eliminate(jnp.concatenate([gram, turned], 1)) * math.sqrt(2 * S)
    count = q_ref.shape[0]
    start = pl.multiple_of(place_ref[1] * count, count)
    q_ref[...] = all_rows[pl.ds(start, count)]


VMEM = pl.BlockSpec(memory_space=pltpu.VMEM)
SMEM = pl.BlockSpec(memory_space=pltpu.SMEM)
ANY = pl.BlockSpec(memory_space=pl.ANY)
HBM = pl.BlockSpec(memory_space=pltpu.HBM)


def call(kernel, outs, specs, *operands, out_specs=None, scratch=(), aliases={}, flops=10**9):
    return pl.pallas_call(
        kernel,
        out_shape=[
            (pltpu.HBM if spec is HBM else jax.ShapeDtypeStruct)(shape, kind)
            for (shape, kind), spec in zip(outs, out_specs or [VMEM] * len(outs))
        ],
        in_specs=specs,
        out_specs=out_specs or [VMEM] * len(outs),
        scratch_shapes=list(scratch),
        input_output_aliases=aliases,
        compiler_params=pltpu.CompilerParams(vmem_limit_bytes=VMEM_LIMIT),
        cost_estimate=pl.CostEstimate(
            flops=flops, bytes_accessed=2**20, transcendentals=0
        ),
    )(*operands)


def in_hbm(block):
    return pltpu.with_memory_space_constraint(block, pltpu.HBM)


def swap(block, even, odd):
    leaves, reps = lax.axis_size("leaf"), lax.axis_size("rep")
    route = [
        (i * reps + j, i * reps + (j ^ (odd if i % 2 else even)))
        for i in range(leaves)
        for j in range(reps)
    ]
    return lax.ppermute(block, ("leaf", "rep"), route)


def cross(block, mask):
    count = lax.axis_size("leaf")
    return lax.ppermute(block, "leaf", [(i, i ^ mask) for i in range(count)])


def body(curve_coordinates, weighted_density, random_test_matrix, sketch_matrix):
    columns, width = random_test_matrix.shape
    cells = width // LEAF
    cell_levels = cells.bit_length() - 1
    rep = lax.axis_index("rep").astype(jnp.int32)
    leaf = lax.axis_index("leaf").astype(jnp.int32)
    count = lax.axis_size("leaf")
    turned = leaf & 1
    own = turn(rep, turned)

    density = weighted_density[None]

    def edge(rows, last):
        return pl.BlockSpec((rows, LEAF), lambda i: (0, cells - 1 if last else 0))

    low, high = pl.pallas_call(
        edges_kernel,
        grid=(1,),
        out_shape=[jax.ShapeDtypeStruct((2 * SUB, LEAF), F32)] * 2,
        in_specs=[edge(columns, False), edge(columns, True), edge(2, False), edge(2, True)]
        + [pl.BlockSpec((1, width), lambda i: (0, 0))],
        out_specs=[pl.BlockSpec((2 * SUB, LEAF), lambda i: (0, 0))] * 2,
    )(random_test_matrix, random_test_matrix, curve_coordinates, curve_coordinates, density)
    low = lax.ppermute(low, "leaf", [(i, (i + 1) % count) for i in range(count)])
    high = lax.ppermute(high, "leaf", [(i, (i - 1) % count) for i in range(count)])

    (parcels,) = call(
        pack_kernel,
        [((cells, 4, columns, LEAF), F32)],
        [SMEM, HBM, HBM],
        turned.reshape(1),
        in_hbm(sketch_matrix),
        in_hbm(random_test_matrix),
        out_specs=[HBM],
        scratch=[
            pltpu.VMEM((columns, width), F32),
            pltpu.VMEM((columns, width), F32),
            pltpu.SemaphoreType.DMA((2,)),
            pltpu.SemaphoreType.DMA((4 * cells - 2,)),
        ],
    )
    (parcels,) = call(
        ends_kernel,
        [((cells, 4, columns, LEAF), F32)],
        [HBM, HBM, HBM],
        parcels,
        low,
        high,
        out_specs=[HBM],
        scratch=[pltpu.SemaphoreType.DMA((2,))],
        aliases={0: 0},
        flops=10**6,
    )
    data = lax.all_to_all(parcels, "rep", 0, 0)

    near_high, near_mid, far, *pairs = call(
        prepare_kernel,
        [((3 * LEAF, LEAF), BF16)] * 2
        + [((SUB, S), F32)]
        + [((2, S, S), F32)] * cell_levels,
        [SMEM] + [VMEM] * 4,
        own.reshape(1),
        curve_coordinates,
        density,
        low,
        high,
        scratch=[
            pltpu.VMEM((SUB, width + 2 * LEAF), F32),
            pltpu.VMEM((SUB, 3 * LEAF), F32),
            pltpu.VMEM((cells, SUB, S), F32),
            pltpu.VMEM((3 * LEAF, LEAF), BF16),
            pltpu.SemaphoreType.DMA,
        ],
        out_specs=[VMEM, HBM] + [VMEM] * (cell_levels + 1),
        flops=10**10,
    )
    skeleton = far
    for level in range(3):
        pair, *joined = call(
            far_kernel,
            [((2, S, S), F32), ((SUB, S), F32)][: 2 - level // 2],
            [SMEM] + [VMEM] * 2,
            (leaf >> level & 1).reshape(1),
            skeleton,
            cross(skeleton, 1 << level),
        )
        pairs.append(pair)
        skeleton = joined[0] if joined else None

    z, inverse, hat = call(
        leaf_kernel,
        [((S, LEAF), F32), ((S, S), F32), ((2 * S, S), F32)],
        [VMEM, VMEM, HBM, ANY],
        data,
        near_high,
        in_hbm(near_mid),
        pairs[-2],
        scratch=[pltpu.VMEM((3 * LEAF, LEAF), BF16), pltpu.SemaphoreType.DMA((3,))],
    )
    (basis,) = call(
        basis_kernel, [((cells, columns, LEAF), F32)], [VMEM] * 2, inverse, z
    )
    parts = lax.all_to_all(basis, "rep", 0, 0)

    for level, masks in enumerate(((1, 4), (3, 12), (4, 1), (12, 3))):
        pair = pairs[level]
        (hat,) = call(
            parent_kernel,
            [((2 * S, S), F32)],
            [VMEM] * 3 + [ANY] * (level == 1),
            pair,
            hat,
            swap(hat, *masks),
            *pairs[-1:] * (level == 1),
        )
    (hat,) = call(
        parent_kernel, [((2 * S, S), F32)], [VMEM] * 3, pairs[-3], hat, cross(hat, 1)
    )
    hat, half = call(
        last_parent_kernel,
        [((2 * S, S), F32), ((S, S), F32)],
        [SMEM] + [VMEM] * 3,
        turned.reshape(1),
        pairs[-2],
        hat,
        cross(hat, 2),
    )
    direct = cross(half, 4)
    (top,) = call(
        top_kernel,
        [((columns, 2 * S), F32)],
        [SMEM] + [VMEM] * 4,
        jnp.stack([leaf >> 2 & 1, rep, turned]),
        pairs[-1],
        hat,
        direct,
        cross(direct, 1),
        scratch=[
            pltpu.VMEM((S, 2 * S), F32),
            pltpu.VMEM((2 * S, S), F32),
        ],
    )
    leaf_basis, top = call(
        lay_kernel,
        [((columns, width), F32), ((columns, 2 * S), F32)],
        [SMEM, VMEM, VMEM],
        turned.reshape(1),
        parts,
        top,
        out_specs=[HBM, HBM],
        scratch=[pltpu.SemaphoreType.DMA((cells + 1,))],
    )
    return (leaf_basis, top[None])


def solution(mesh):
    return jax.shard_map(
        body,
        mesh=mesh,
        in_specs=(P(None, "leaf"), P("leaf"), P("rep", "leaf"), P("rep", "leaf")),
        out_specs=(P("rep", "leaf"), P("leaf", "rep", None)),
        check_vma=False,
    )
```

```python
import math

import jax
import jax.numpy as jnp
from jax import lax
from jax.experimental import pallas as pl
from jax.experimental.pallas import tpu as pltpu
from jax.sharding import PartitionSpec as P

LEAF = 512
S = 128
NB = 32
SUB = 8
STEP = LEAF // S
F32 = jnp.float32
BF16 = jnp.bfloat16
LOG_SCALE = -0.25 / math.pi
VMEM_LIMIT = 16 * 1024 * 1024


def split3(x):
    high = x.astype(BF16)
    rest = x - high.astype(F32)
    mid = rest.astype(BF16)
    return high, mid, (rest - mid.astype(F32)).astype(BF16)


def product(a, b, dims):
    ah, am, al = a
    bh, bm, bl = b
    left = jnp.concatenate([ah, ah, am, ah, al, am], dims[0][0])
    right = jnp.concatenate([bh, bm, bh, bl, bh, bm], dims[1][0])
    return lax.dot_general(left, right, (dims, ((), ())), preferred_element_type=F32)


def nn(a, b):
    return product(a, b, ((1,), (0,)))


def nt(a, b):
    return product(a, b, ((1,), (1,)))


def tn(a, b):
    return product(a, b, ((0,), (0,)))


def block_rows(diagonal, rows):
    n, width = rows.shape
    groups = n // SUB
    tiles = width // S
    sub = lax.broadcasted_iota(jnp.int32, (SUB, S), 0)
    cols = [
        [
            jnp.broadcast_to(diagonal[SUB * g : SUB * (g + 1), j : j + 1], (SUB, S))
            if g >= j // SUB
            else None
            for g in range(groups)
        ]
        for j in range(n)
    ]
    work = [
        [rows[SUB * g : SUB * (g + 1), S * t : S * (t + 1)] for t in range(tiles)]
        for g in range(groups)
    ]
    scales = [jnp.zeros((SUB, S), F32)] * groups
    factors = []

    def update(j, k):
        gj, sj = divmod(j, SUB)
        other = factors[k][gj][sj : sj + 1]
        for g in range(gj, groups):
            cols[j][g] = cols[j][g] - factors[k][g] * other

    for k in range(n):
        gk, sk = divmod(k, SUB)
        scale = lax.rsqrt(jnp.broadcast_to(cols[k][gk][sk : sk + 1], (SUB, S)))
        factor = {g: cols[k][g] * scale for g in range(gk, groups)}
        factors.append(dict(factor))
        scales[gk] = jnp.where(sub == sk, scale, scales[gk])
        if k + 1 < n:
            update(k + 1, k)
        if k + 2 < n:
            for earlier in range(k + 1):
                update(k + 2, earlier)
        factor[gk] = jnp.where(sub > sk, factor[gk], 0.0)
        for t in range(tiles):
            pivot_row = work[gk][t][sk : sk + 1] * scale
            for g in range(gk + (sk == SUB - 1), groups):
                work[g][t] = work[g][t] - factor[g] * pivot_row
    return jnp.concatenate(
        [
            jnp.concatenate([tile * scales[g] for tile in work[g]], 1)
            for g in range(groups)
        ],
        0,
    )


def eliminate(whole):
    n = whole.shape[0]
    blocks = [whole[i : i + NB] for i in range(0, n, NB)]
    done = []
    for k in range(len(blocks)):
        diagonal = blocks[k][:, k * NB : (k + 1) * NB]
        if k == len(blocks) - 1:
            done.append(block_rows(diagonal, blocks[k][:, n:]))
            break
        upper = block_rows(diagonal, blocks[k])
        done.append(upper[:, n:])
        parts = split3(upper)
        for j in range(k + 1, len(blocks)):
            at = slice(j * NB, (j + 1) * NB)
            blocks[j] = blocks[j] - tn([p[:, at] for p in parts], parts)
    return jnp.concatenate(done, 0)


def squared_distances(cols, rows):
    dx = cols[:, 0:1] - rows[0:1]
    dy = cols[:, 1:2] - rows[1:2]
    return dx * dx + dy * dy


def pick(x, every):
    n, width = x.shape
    kept = width // every
    i = lax.broadcasted_iota(jnp.int32, (width, kept), 0)
    j = lax.broadcasted_iota(jnp.int32, (width, kept), 1)
    chosen = jnp.where(i == every * j, 1.0, 0.0).astype(BF16)
    parts = jnp.concatenate([p.astype(F32) for p in split3(x)], 0).astype(BF16)
    got = jnp.dot(parts, chosen, preferred_element_type=F32)
    return got[:n] + (got[n : 2 * n] + got[2 * n :])


def coupling(mine, other, scale):
    to_mine = jnp.log(squared_distances(mine.T, other)) * (other[2:3] * scale)
    to_other = jnp.log(squared_distances(other.T, mine)) * (mine[2:3] * scale)
    return to_mine, to_other


def prepare_kernel(
    rep_ref, coords_ref, density_ref, low_ref, high_ref,
    near_high_ref, near_mid_hbm, far_ref, *rest,
):
    pair_refs, (wide, window, skeleton, near_mid_ref, sem) = rest[:-5], rest[-5:]
    rep = rep_ref[0]
    width = coords_ref.shape[1]
    cells = width // LEAF
    wide[:, :LEAF] = low_ref[SUB:]
    wide[:2, LEAF : LEAF + width] = coords_ref[...]
    wide[2:3, LEAF : LEAF + width] = density_ref[...]
    wide[3:, LEAF : LEAF + width] = jnp.zeros((SUB - 3, width), F32)
    wide[:, LEAF + width :] = high_ref[SUB:]

    window[...] = wide[:, pl.ds(pl.multiple_of(rep * LEAF, LEAF), 3 * LEAF)]
    targets = window[:, LEAF : 2 * LEAF]

    def near_chunk(chunk, carry):
        at = pl.ds(pl.multiple_of(chunk * S, S), S)
        cols = window[:, at].T
        i = lax.broadcasted_iota(jnp.int32, (S, LEAF), 0) + (chunk * S - LEAF)
        same = i == lax.broadcasted_iota(jnp.int32, (S, LEAF), 1)
        squared = jnp.where(same, 1.0, squared_distances(cols, targets))
        itself = -2.0 * (1.0 - jnp.log(0.5 * cols[:, 2:3]))
        values = jnp.where(same, itself, jnp.log(squared)) * (cols[:, 2:3] * LOG_SCALE)
        high = values.astype(BF16)
        near_high_ref[at] = high
        near_mid_ref[at] = (values - high.astype(F32)).astype(BF16)
        return carry

    lax.fori_loop(0, 3 * LEAF // S, near_chunk, 0)
    store = pltpu.make_async_copy(near_mid_ref, near_mid_hbm, sem)
    store.start()

    leaves = [wide[:, LEAF * (i + 1) : LEAF * (i + 2)] for i in range(cells)]
    nodes = pick(jnp.concatenate(leaves, 0), STEP)
    for level, ref in enumerate(pair_refs):
        count = cells >> level
        for i in range(count):
            skeleton[i] = nodes[SUB * i : SUB * (i + 1)]
        index = rep >> level
        pair = coupling(
            skeleton[index], skeleton[index ^ 1], LOG_SCALE * (STEP << level)
        )
        for side in range(2):
            ref[side] = pair[side]
        joined = [
            jnp.concatenate(
                [nodes[SUB * i : SUB * (i + 1)], nodes[SUB * (i + 1) : SUB * (i + 2)]], 1
            )
            for i in range(0, count, 2)
        ]
        nodes = pick(jnp.concatenate(joined, 0), 2)
    scale = jnp.where(
        lax.broadcasted_iota(jnp.int32, (SUB, S), 0) == 2,
        float(STEP << len(pair_refs)), 1.0,
    )
    far_ref[...] = nodes * scale
    store.wait()


def edges_kernel(
    first_ref, last_ref, first_coords_ref, last_coords_ref, density_ref, low_ref, high_ref
):
    width = density_ref.shape[1]
    sides = (
        (high_ref, first_ref, first_coords_ref, 0),
        (low_ref, last_ref, last_coords_ref, width - LEAF),
    )
    for ref, tests_ref, coords_ref, start in sides:
        ref[:SUB] = tests_ref[...]
        ref[SUB : SUB + 2] = coords_ref[...]
        ref[SUB + 2 : SUB + 3] = density_ref[:, start : start + LEAF]
        ref[SUB + 3 :] = jnp.zeros((SUB - 3, LEAF), F32)


def turn(index, turned):
    return jnp.where(turned == 1, index % 4 * 4 + index // 4, index)


def pack_kernel(turned_ref, samples_hbm, tests_hbm, out_ref, samples_ref, tests_ref, ins, sems):
    cells = out_ref.shape[0]
    loads = [
        pltpu.make_async_copy(samples_hbm, samples_ref, ins.at[0]),
        pltpu.make_async_copy(tests_hbm, tests_ref, ins.at[1]),
    ]
    for load in loads:
        load.start()
    for load in loads:
        load.wait()
    copies = []

    def move(source, leaf, i, slot):
        start = pl.multiple_of(leaf * LEAF, LEAF)
        copies.append(
            pltpu.make_async_copy(
                source.at[:, pl.ds(start, LEAF)], out_ref.at[i, slot], sems.at[len(copies)]
            )
        )
        copies[-1].start()

    for i in range(cells):
        leaf = turn(jnp.int32(i), turned_ref[0])
        move(samples_ref, leaf, i, 0)
        if i > 0:
            move(tests_ref, leaf - 1, i, 1)
        move(tests_ref, leaf, i, 2)
        if i < cells - 1:
            move(tests_ref, leaf + 1, i, 3)
    for copy in copies:
        copy.wait()


def ends_kernel(packed_ref, low_ref, high_ref, out_ref, sems):
    copies = [
        pltpu.make_async_copy(low_ref.at[:SUB], out_ref.at[0, 1], sems.at[0]),
        pltpu.make_async_copy(
            high_ref.at[:SUB], out_ref.at[out_ref.shape[0] - 1, 3], sems.at[1]
        ),
    ]
    for copy in copies:
        copy.start()
    for copy in copies:
        copy.wait()


def leaf_kernel(
    data_ref, near_high_ref, near_mid_hbm, _, z_ref, inverse_ref, hat_ref, near_mid_ref, sems
):
    pieces = [pl.ds(part * LEAF, LEAF) for part in range(3)]
    fetches = [
        pltpu.make_async_copy(near_mid_hbm.at[at], near_mid_ref.at[at], sems.at[i])
        for i, at in enumerate(pieces)
    ]
    for fetch in fetches:
        fetch.start()
    near = jnp.zeros((S, LEAF), F32)
    highs = []
    for part in range(3):
        near_high = near_high_ref[part * LEAF : (part + 1) * LEAF]
        high, mid, _ = split3(data_ref[:, part + 1].reshape(S, LEAF))
        left = jnp.concatenate([high, mid], 1)
        right = jnp.concatenate([near_high, near_high], 0)
        near = near + jnp.dot(left, right, preferred_element_type=F32)
        highs.append(high)
    for fetch in fetches:
        fetch.wait()
    near = near + jnp.dot(
        jnp.concatenate(highs, 1), near_mid_ref[...], preferred_element_type=F32
    )
    samples = data_ref[:, 0].reshape(S, LEAF)
    z = samples - near
    z_ref[...] = z
    parts = split3(z)
    both = [split3(samples), split3(data_ref[:, 2].reshape(S, LEAF))]
    gram = nt(parts, parts)
    rights = [nt(parts, x) for x in both]
    eye = jnp.where(
        lax.broadcasted_iota(jnp.int32, (S, S), 0) == lax.broadcasted_iota(jnp.int32, (S, S), 1),
        1.0, 0.0,
    ).astype(F32)
    got = eliminate(jnp.concatenate([gram, *rights, eye], 1))
    hat_ref[:S] = got[:, :S]
    hat_ref[S:] = got[:, S : 2 * S]
    inverse_ref[...] = got[:, 2 * S :]


def basis_kernel(inverse_ref, z_ref, q_ref):
    q = nn(split3(inverse_ref[...]), split3(z_ref[...])) * math.sqrt(LEAF)
    q_ref[...] = q.reshape(q_ref.shape)


def off_diagonal(to_mine, to_other, mine_ref, other_ref):
    z_mine = mine_ref[:S] - nn(to_mine, split3(other_ref[S : 2 * S]))
    z_other = other_ref[:S] - nn(to_other, split3(mine_ref[S : 2 * S]))
    return z_mine, z_other


def merge(to_mine, to_other, mine_ref, other_ref):
    z_mine, z_other = off_diagonal(to_mine, to_other, mine_ref, other_ref)
    left = split3(jnp.concatenate([z_mine.T, z_other.T], 1))
    mine = jnp.concatenate([z_mine, mine_ref[:S], mine_ref[S : 2 * S]], 1)
    other = jnp.concatenate([z_other, other_ref[:S], other_ref[S : 2 * S]], 1)
    return eliminate(nn(left, split3(jnp.concatenate([mine, other], 0))))


def far_kernel(second_ref, mine_ref, other_ref, pair_ref, *joined_refs):
    mine, other = mine_ref[...], other_ref[...]
    for side, block in enumerate(coupling(mine, other, LOG_SCALE)):
        pair_ref[side] = block
    second = second_ref[0] == 1
    joined = jnp.concatenate(
        [jnp.where(second, other, mine), jnp.where(second, mine, other)], 1
    )
    double = lax.broadcasted_iota(jnp.int32, (SUB, S), 0) == 2
    for ref in joined_refs:
        ref[...] = pick(joined, 2) * jnp.where(double, 2.0, 1.0)


def parent_kernel(pair_ref, mine_ref, other_ref, *rest):
    hat_ref = rest[-1]
    pair = [split3(pair_ref[side]) for side in range(2)]
    got = merge(*pair, mine_ref, other_ref)
    hat_ref[:S] = got[:, :S]
    hat_ref[S:] = got[:, S:]


def lay_kernel(turned_ref, parts_ref, basis_ref, sems):
    copies = []
    for i in range(parts_ref.shape[0]):
        leaf = turn(jnp.int32(i), turned_ref[0])
        to = basis_ref.at[:, pl.ds(pl.multiple_of(leaf * LEAF, LEAF), LEAF)]
        copies.append(pltpu.make_async_copy(parts_ref.at[i], to, sems.at[i]))
        copies[-1].start()
    for copy in copies:
        copy.wait()


def last_parent_kernel(turned_ref, pair_ref, mine_ref, other_ref, hat_ref, half_ref):
    parent_kernel(pair_ref, mine_ref, other_ref, hat_ref)
    half_ref[...] = jnp.where(turned_ref[0] == 1, hat_ref[S:], hat_ref[:S])


def top_kernel(
    place_ref, pair_ref, mine_ref, direct_ref, passed_ref, _, q_ref, all_rows, other_ref
):
    upper_direct = place_ref[2] == 0
    other_ref[:S] = jnp.where(upper_direct, direct_ref[...], passed_ref[...])
    other_ref[S:] = jnp.where(upper_direct, passed_ref[...], direct_ref[...])
    pair = [split3(pair_ref[side]) for side in range(2)]
    z_mine, z_other = off_diagonal(*pair, mine_ref, other_ref)
    second = place_ref[0] == 1
    first = jnp.where(second, z_other, z_mine)
    last = jnp.where(second, z_mine, z_other)
    turned = jnp.concatenate([first.T, last.T], 1)
    gram = nn(split3(turned), split3(jnp.concatenate([first, last], 0)))
    all_rows[...] = eliminate(jnp.concatenate([gram, turned], 1)) * math.sqrt(2 * S)
    count = q_ref.shape[0]
    start = pl.multiple_of(place_ref[1] * count, count)
    q_ref[...] = all_rows[pl.ds(start, count)]


VMEM = pl.BlockSpec(memory_space=pltpu.VMEM)
SMEM = pl.BlockSpec(memory_space=pltpu.SMEM)
ANY = pl.BlockSpec(memory_space=pl.ANY)
HBM = pl.BlockSpec(memory_space=pltpu.HBM)


def call(kernel, outs, specs, *operands, out_specs=None, scratch=(), aliases={}, flops=10**9):
    return pl.pallas_call(
        kernel,
        out_shape=[
            (pltpu.HBM if spec is HBM else jax.ShapeDtypeStruct)(shape, kind)
            for (shape, kind), spec in zip(outs, out_specs or [VMEM] * len(outs))
        ],
        in_specs=specs,
        out_specs=out_specs or [VMEM] * len(outs),
        scratch_shapes=list(scratch),
        input_output_aliases=aliases,
        compiler_params=pltpu.CompilerParams(vmem_limit_bytes=VMEM_LIMIT),
        cost_estimate=pl.CostEstimate(
            flops=flops, bytes_accessed=2**20, transcendentals=0
        ),
    )(*operands)


def in_hbm(block):
    return pltpu.with_memory_space_constraint(block, pltpu.HBM)


def swap(block, even, odd):
    leaves, reps = lax.axis_size("leaf"), lax.axis_size("rep")
    route = [
        (i * reps + j, i * reps + (j ^ (odd if i % 2 else even)))
        for i in range(leaves)
        for j in range(reps)
    ]
    return lax.ppermute(block, ("leaf", "rep"), route)


def cross(block, mask):
    count = lax.axis_size("leaf")
    return lax.ppermute(block, "leaf", [(i, i ^ mask) for i in range(count)])


def body(curve_coordinates, weighted_density, random_test_matrix, sketch_matrix):
    columns, width = random_test_matrix.shape
    cells = width // LEAF
    cell_levels = cells.bit_length() - 1
    rep = lax.axis_index("rep").astype(jnp.int32)
    leaf = lax.axis_index("leaf").astype(jnp.int32)
    count = lax.axis_size("leaf")
    turned = leaf & 1
    own = turn(rep, turned)

    density = weighted_density[None]

    def edge(rows, last):
        return pl.BlockSpec((rows, LEAF), lambda i: (0, cells - 1 if last else 0))

    low, high = pl.pallas_call(
        edges_kernel,
        grid=(1,),
        out_shape=[jax.ShapeDtypeStruct((2 * SUB, LEAF), F32)] * 2,
        in_specs=[edge(columns, False), edge(columns, True), edge(2, False), edge(2, True)]
        + [pl.BlockSpec((1, width), lambda i: (0, 0))],
        out_specs=[pl.BlockSpec((2 * SUB, LEAF), lambda i: (0, 0))] * 2,
    )(random_test_matrix, random_test_matrix, curve_coordinates, curve_coordinates, density)
    low = lax.ppermute(low, "leaf", [(i, (i + 1) % count) for i in range(count)])
    high = lax.ppermute(high, "leaf", [(i, (i - 1) % count) for i in range(count)])

    (parcels,) = call(
        pack_kernel,
        [((cells, 4, columns, LEAF), F32)],
        [SMEM, HBM, HBM],
        turned.reshape(1),
        in_hbm(sketch_matrix),
        in_hbm(random_test_matrix),
        out_specs=[HBM],
        scratch=[
            pltpu.VMEM((columns, width), F32),
            pltpu.VMEM((columns, width), F32),
            pltpu.SemaphoreType.DMA((2,)),
            pltpu.SemaphoreType.DMA((4 * cells - 2,)),
        ],
    )
    (parcels,) = call(
        ends_kernel,
        [((cells, 4, columns, LEAF), F32)],
        [HBM, HBM, HBM],
        parcels,
        low,
        high,
        out_specs=[HBM],
        scratch=[pltpu.SemaphoreType.DMA((2,))],
        aliases={0: 0},
        flops=10**6,
    )
    data = lax.all_to_all(parcels, "rep", 0, 0)

    near_high, near_mid, far, *pairs = call(
        prepare_kernel,
        [((3 * LEAF, LEAF), BF16)] * 2
        + [((SUB, S), F32)]
        + [((2, S, S), F32)] * cell_levels,
        [SMEM] + [VMEM] * 4,
        own.reshape(1),
        curve_coordinates,
        density,
        low,
        high,
        scratch=[
            pltpu.VMEM((SUB, width + 2 * LEAF), F32),
            pltpu.VMEM((SUB, 3 * LEAF), F32),
            pltpu.VMEM((cells, SUB, S), F32),
            pltpu.VMEM((3 * LEAF, LEAF), BF16),
            pltpu.SemaphoreType.DMA,
        ],
        out_specs=[VMEM, HBM] + [VMEM] * (cell_levels + 1),
        flops=10**10,
    )
    skeleton = far
    for level in range(3):
        pair, *joined = call(
            far_kernel,
            [((2, S, S), F32), ((SUB, S), F32)][: 2 - level // 2],
            [SMEM] + [VMEM] * 2,
            (leaf >> level & 1).reshape(1),
            skeleton,
            cross(skeleton, 1 << level),
        )
        pairs.append(pair)
        skeleton = joined[0] if joined else None

    z, inverse, hat = call(
        leaf_kernel,
        [((S, LEAF), F32), ((S, S), F32), ((2 * S, S), F32)],
        [VMEM, VMEM, HBM, ANY],
        data,
        near_high,
        in_hbm(near_mid),
        pairs[-2],
        scratch=[pltpu.VMEM((3 * LEAF, LEAF), BF16), pltpu.SemaphoreType.DMA((3,))],
    )
    (basis,) = call(
        basis_kernel, [((cells, columns, LEAF), F32)], [VMEM] * 2, inverse, z
    )
    parts = lax.all_to_all(basis, "rep", 0, 0)

    for level, masks in enumerate(((1, 4), (3, 12), (4, 1), (12, 3))):
        pair = pairs[level]
        (hat,) = call(
            parent_kernel,
            [((2 * S, S), F32)],
            [VMEM] * 3 + [ANY] * (level == 1),
            pair,
            hat,
            swap(hat, *masks),
            *pairs[-1:] * (level == 1),
        )
    (hat,) = call(
        parent_kernel, [((2 * S, S), F32)], [VMEM] * 3, pairs[-3], hat, cross(hat, 1)
    )
    hat, half = call(
        last_parent_kernel,
        [((2 * S, S), F32), ((S, S), F32)],
        [SMEM] + [VMEM] * 3,
        turned.reshape(1),
        pairs[-2],
        hat,
        cross(hat, 2),
    )
    direct = cross(half, 4)
    (leaf_basis,) = call(
        lay_kernel,
        [((columns, width), F32)],
        [SMEM, VMEM],
        turned.reshape(1),
        parts,
        out_specs=[HBM],
        scratch=[pltpu.SemaphoreType.DMA((cells,))],
    )
    (top,) = call(
        top_kernel,
        [((columns, 2 * S), F32)],
        [SMEM] + [VMEM] * 4 + [HBM],
        jnp.stack([leaf >> 2 & 1, rep, turned]),
        pairs[-1],
        hat,
        direct,
        cross(direct, 1),
        in_hbm(leaf_basis),
        scratch=[
            pltpu.VMEM((S, 2 * S), F32),
            pltpu.VMEM((2 * S, S), F32),
        ],
    )
    return (leaf_basis, top[None])


def solution(mesh):
    return jax.shard_map(
        body,
        mesh=mesh,
        in_specs=(P(None, "leaf"), P("leaf"), P("rep", "leaf"), P("rep", "leaf")),
        out_specs=(P("rep", "leaf"), P("leaf", "rep", None)),
        check_vma=False,
    )
```
